32 devices in a mesh: seq: 8 (over z, x), head: 4 (over y, core).
Axes of the slice: x: 2, y: 2, z: 4, core: 2. Of those that a mesh axis runs over, the one named last changes fastest.
Arguments:
- features_in: bfloat16 [4096, 3072], P('seq', 'head'), may hold values from -66 to 66
- gate_in: bfloat16 [4096, 3072], P('seq', 'head'), may hold values from -6 to 6
- b_input: bfloat16 [4096, 128], P('seq'), may hold values from -0.0234375 to 0.0234375
- c_input: bfloat16 [4096, 128], P('seq'), may hold values from -6 to 6
- log_decay: bfloat16 [4096, 48], P('seq', 'head'), may hold values from -1 to 0, as said below
- row_target: int32 [4096], P('seq'), may hold values from 0 to 4095, as said below
- doc_lengths: int32 [4], replicated, may hold values from 1 to 2048, 4096 in all
- skip_gain: float32 [48], P('head'), may hold values from 0.5 to 1.5
- norm_gain: float32 [3072], P('head'), may hold values from 0.1 to 1.9
- out_weight: bfloat16 [3072, 1536], P('head'), may hold values from -0.109375 to 0.109375
Outputs:
- layer_out: bfloat16 [4096, 1536], P(('seq', 'head'))
The draws below stay inside these ranges and needn't reach their ends.
Inputs may be any that keep to these rules, and one draw needn't show every extreme that they name: row_target is a permutation; the rows of one device go to every device along seq, exactly 64 rows to each. `doc_lengths`: the lengths sum to 4096. `log_decay`: every decay is below one.
All inputs are finite; a program needn't handle non-finite values.
Results may differ from the reference program's by a relative error of at most 0.022.
Values may be sent and summed in bfloat16 or wider, within the bound.
A program may use at most 128 MiB of HBM per device.

```python
import math
import jax
import jax.numpy as jnp
import numpy as np
from jax import lax

D_MODEL = 1536
ATTENTION_LANES = 48
HEAD_DIM = 64
STATE = 128
TOK_DEV = 512
BLOCK = 512
DOCS = 4
GROUP_HEADS = 12
GROUPS = 8
CAP = 64
STACKED_SPOTS = 4096
MOST_DOC = 2048


def shuffle_one(sub_key):
    return jax.random.permutation(sub_key, TOK_DEV)


def make_targets(key):
    key = jax.random.fold_in(key, 17)
    lookup_series = jax.random.split(key, 3)
    shards = STACKED_SPOTS // TOK_DEV
    offsets = jax.random.permutation(lookup_series[0], shards)[:GROUPS].astype(jnp.int32)
    slots = jnp.arange(TOK_DEV, dtype=jnp.int32)
    sources = jnp.arange(shards, dtype=jnp.int32)[:, None]
    target_dev = (sources - offsets[slots // CAP][None, :]) % shards
    shuffle_in = jax.vmap(shuffle_one)(jax.random.split(lookup_series[1], shards)).astype(jnp.int32)
    shuffle_out = jax.vmap(shuffle_one)(jax.random.split(lookup_series[2], shards)).astype(jnp.int32)
    target = target_dev * TOK_DEV + shuffle_out[target_dev, slots[None, :]]
    row_table = jnp.zeros((shards, TOK_DEV), jnp.int32).at[sources, shuffle_in].set(target)
    return row_table.reshape(STACKED_SPOTS)


def draw_row_target(key, part):
    return make_targets(key)


def draw_log_decay(key, part):
    targets = make_targets(key)
    key = jax.random.fold_in(key, 23)
    lookup_series = jax.random.split(key, 7)
    fast_share = 0.5
    fast_head = jax.random.uniform(lookup_series[0], (ATTENTION_LANES,)) < fast_share
    fast_rate = jnp.exp(jax.random.uniform(lookup_series[1], (ATTENTION_LANES,), minval=math.log(1.0 / 50.0), maxval=math.log(1.0 / 30.0)))
    slow_rate = jnp.exp(jax.random.uniform(lookup_series[2], (ATTENTION_LANES,), minval=math.log(0.03), maxval=math.log(0.25))) / STACKED_SPOTS
    head_rate = jnp.where(fast_head, fast_rate, slow_rate)
    roughness = jnp.exp(jax.random.uniform(lookup_series[3], (STACKED_SPOTS, ATTENTION_LANES), minval=math.log(0.5), maxval=math.log(2.0)))
    region = jnp.exp(jax.random.uniform(lookup_series[4], (STACKED_SPOTS // TOK_DEV,), minval=math.log(0.5), maxval=math.log(2.0)))
    concatenated_symbols = -head_rate[None, :] * roughness * jnp.repeat(region, TOK_DEV)[:, None]
    spike_location = jax.random.randint(lookup_series[5], (3,), 0, STACKED_SPOTS)
    spike_surcharge = jax.random.uniform(lookup_series[6], (3, ATTENTION_LANES), minval=0.2, maxval=0.5)
    concatenated_symbols = concatenated_symbols.at[spike_location].set(jnp.log(1.0 - spike_surcharge))
    return concatenated_symbols[targets].astype(jnp.bfloat16)


def draw_features_in(key, part):
    key = jax.random.fold_in(key, 31)
    lookup_series = jax.random.split(key, 3)
    columns = ATTENTION_LANES * HEAD_DIM
    head_number = (jnp.arange(columns) // HEAD_DIM).astype(jnp.float32)
    base_draw = jnp.clip(jax.random.normal(lookup_series[0], (STACKED_SPOTS, columns)), -4.0, 4.0)
    head_rise = 3.0 ** (head_number / (ATTENTION_LANES - 1))
    roughness = jnp.exp(jax.random.uniform(lookup_series[1], (columns,), minval=-0.6, maxval=0.6))
    row_scale = jnp.exp(jax.random.uniform(lookup_series[2], (STACKED_SPOTS, 1), minval=math.log(0.3), maxval=math.log(3.0)))
    return (base_draw * row_scale * head_rise[None, :] * roughness[None, :]).astype(jnp.bfloat16)


def block_scale(stream_key, dims, cuts, least, top_value):
    level = 1.0
    for dim, parts in cuts:
        heights = jax.random.uniform(jax.random.fold_in(jax.random.fold_in(stream_key, 6), dim), (parts,), jnp.float32, least / len(cuts), top_value / len(cuts))
        level = level * jnp.repeat(jnp.exp(heights), dims[dim] // parts).reshape((-1,) + (1,) * (len(dims) - 1 - dim))
    return level


def profile(amount, total, most, skew):
    loads = [(1 << 20) // math.isqrt(standing ** skew) + 1 for standing in range(2, amount + 1)]
    rest, counts = total - most - (amount - 1), [1] * (amount - 1)
    while rest > 0:
        free = [i for i in range(amount - 1) if counts[i] < most]
        pool, budget = sum([loads[i] for i in free]), rest
        for i in free:
            extra = min(most - counts[i], max(1, budget * loads[i] // pool), rest)
            counts[i] = counts[i] + extra
            rest = rest - extra
    return np.array([most] + counts)


def ragged_sizes(stream_key, amount, total, most, slope):
    if amount == 2:
        one = jax.random.randint(stream_key, (), max(1, total - most), min(most, total - 1) + 1)
        return jnp.stack([one, total - one])
    sizes = jnp.asarray(profile(amount, total, most, slope), jnp.int32)
    couples = (amount - 1) // 2
    giver, sink = sizes[1:1 + 2 * couples:2], sizes[2:2 + 2 * couples:2]
    slack = jnp.minimum(giver - 1, most - sink)
    moved = jax.random.randint(jax.random.fold_in(stream_key, 1), (couples,), 0, 1 << 20) % (slack + 1)
    sizes = sizes.at[1:1 + 2 * couples:2].set(giver - moved).at[2:2 + 2 * couples:2].set(sink + moved)
    return sizes[jax.random.permutation(jax.random.fold_in(stream_key, 2), amount)]


def centred(stream_key, shape, deviation, most, cuts=(), kind=jnp.bfloat16):
    array = deviation * jax.random.normal(stream_key, shape, jnp.float32)
    if cuts:
        array = array * block_scale(stream_key, shape, cuts, -0.22, 0.18)
    return jnp.clip(array, -most, most).astype(kind)


def setup_inputs(seed: int = 0) -> dict:
    key_list = jax.random.split(jax.random.key(seed), 11)
    return {
        "features_in": draw_features_in(jax.random.fold_in(key_list[10], 71), 0),
        "gate_in": centred(key_list[1], (STACKED_SPOTS, ATTENTION_LANES * HEAD_DIM), 1.0, 6.0, ((0, 8), (1, 4))),
        "b_input": centred(key_list[2], (STACKED_SPOTS, STATE), (STATE * TOK_DEV) ** -0.5, 0.0234375, ((0, 8),)),
        "c_input": centred(key_list[3], (STACKED_SPOTS, STATE), 1.0, 6.0, ((0, 8),)),
        "log_decay": draw_log_decay(jax.random.fold_in(key_list[10], 71), 0),
        "row_target": draw_row_target(jax.random.fold_in(key_list[10], 71), 0),
        "doc_lengths": ragged_sizes(key_list[6], DOCS, STACKED_SPOTS, MOST_DOC, 1).astype(jnp.int32),
        "skip_gain": jnp.clip(0.5 + 1.0 * jax.random.uniform(key_list[7], (ATTENTION_LANES,), jnp.float32) ** block_scale(key_list[7], (ATTENTION_LANES,), ((0, 4),), -0.2, 0.2), 0.5, 1.5),
        "norm_gain": jnp.clip(1.0 + 0.18 * jax.random.normal(key_list[8], (ATTENTION_LANES * HEAD_DIM,), jnp.float32), 0.1, 1.9),
        "out_weight": centred(key_list[9], (ATTENTION_LANES * HEAD_DIM, D_MODEL), (ATTENTION_LANES * HEAD_DIM) ** -0.5, 0.109375, ((0, 4),)),
    }


far_below = -1e+30
norm_eps = 1e-05

def doc_index(places, starts):
    return (lax.optimization_barrier(jnp.sum((starts[None, :] <= places[:, None]).astype(jnp.int32), axis=1)) - 1).astype(jnp.int32)

def state_terms(by_head, key_block, decay_block, doc_block, before):
    running = jnp.cumsum(decay_block.astype(jnp.float32), axis=0)
    same_doc = (doc_block == doc_block[-1]).astype(jnp.float32)
    closing_weight = jnp.exp(running[-1][None, :] - running) * same_doc[:, None]
    weighted = (key_block.astype(jnp.float32)[None, :, :] * closing_weight.T[:, :, None]).astype(jnp.bfloat16)
    block_state = jnp.einsum('hsn,shp->hpn', weighted.astype(jnp.float32), by_head.astype(jnp.float32))
    through = jnp.exp(running[-1]) * (doc_block[-1] == before).astype(jnp.float32)
    return (block_state, through, running)

def inner_terms(by_head, key_block, query_block, running, doc_block):
    length = running.shape[0]
    later = lax.broadcasted_iota(jnp.int32, (length, length), 0)
    earlier = lax.broadcasted_iota(jnp.int32, (length, length), 1)
    allowed = (later >= earlier) & (doc_block[:, None] == doc_block[None, :])
    running_heads = running.T
    decay_gaps = jnp.where(allowed[None, :, :], running_heads[:, :, None] - running_heads[:, None, :], far_below)
    products = jnp.einsum('tn,sn->ts', query_block.astype(jnp.float32), key_block.astype(jnp.float32))
    affinity_logits = (products[None, :, :] * jnp.exp(decay_gaps)).astype(jnp.bfloat16)
    return jnp.einsum('hts,shp->thp', affinity_logits.astype(jnp.float32), by_head.astype(jnp.float32))

def entry_terms(query_block, carry_state, running, doc_block, before):
    entry_weight = jnp.exp(running) * (doc_block == before).astype(jnp.float32)[:, None]
    carried = jnp.einsum('tn,hpn->thp', query_block.astype(jnp.float32), carry_state, precision=lax.Precision.HIGHEST)
    return carried * entry_weight[:, :, None]

def reference(features_in, gate_in, b_input, c_input, log_decay, row_target, doc_lengths, skip_gain, norm_gain, out_weight):
    source_row = jnp.zeros((STACKED_SPOTS,), jnp.int32).at[row_target].set(jnp.arange(STACKED_SPOTS, dtype=jnp.int32))
    features = features_in[source_row]
    gates = gate_in[source_row]
    key_rows = b_input[source_row]
    query_rows = c_input[source_row]
    decays = log_decay[source_row]
    doc_starts = (jnp.cumsum(doc_lengths) - doc_lengths).astype(jnp.int32)
    blocks = STACKED_SPOTS // BLOCK
    doc_ids = doc_index(jnp.arange(STACKED_SPOTS, dtype=jnp.int32), doc_starts).reshape(blocks, BLOCK)
    doc_before = doc_index(jnp.arange(blocks, dtype=jnp.int32) * BLOCK - 1, doc_starts)
    weights = out_weight.astype(jnp.float32).reshape(ATTENTION_LANES // GROUP_HEADS, GROUP_HEADS * HEAD_DIM, D_MODEL)

    def block_advance(carry_state, pieces):
        incoming_tile, gate_block, key_block, query_block, decay_block, doc_block, before = pieces
        by_head = incoming_tile.reshape(BLOCK, ATTENTION_LANES, HEAD_DIM)
        block_state, through, running = state_terms(by_head, key_block, decay_block, doc_block, before)
        mixed = inner_terms(by_head, key_block, query_block, running, doc_block)
        mixed = mixed + entry_terms(query_block, carry_state, running, doc_block, before)
        mixed = mixed + skip_gain[None, :, None] * by_head.astype(jnp.float32)
        gated = mixed.reshape(BLOCK, ATTENTION_LANES * HEAD_DIM) * jax.nn.silu(gate_block.astype(jnp.float32))
        row_scale = lax.rsqrt(lax.optimization_barrier(jnp.mean(gated * gated, axis=1)) + norm_eps)
        normed = (gated * row_scale[:, None] * norm_gain[None, :]).astype(jnp.bfloat16)
        grouped = normed.astype(jnp.float32).reshape(BLOCK, ATTENTION_LANES // GROUP_HEADS, GROUP_HEADS * HEAD_DIM)
        partial_value = jnp.einsum('tgk,gkd->gtd', grouped, weights).astype(jnp.bfloat16)
        partial_value = lax.optimization_barrier(partial_value)
        out_block = lax.optimization_barrier(jnp.sum(partial_value.astype(jnp.float32), axis=0)).astype(jnp.bfloat16)
        return (through[:, None, None] * carry_state + block_state, out_block)
    start_state = jnp.zeros((ATTENTION_LANES, HEAD_DIM, STATE), jnp.float32)
    final_state, outputs = lax.scan(block_advance, start_state, (features.reshape(blocks, BLOCK, ATTENTION_LANES * HEAD_DIM), gates.reshape(blocks, BLOCK, ATTENTION_LANES * HEAD_DIM), key_rows.reshape(blocks, BLOCK, STATE), query_rows.reshape(blocks, BLOCK, STATE), decays.reshape(blocks, BLOCK, ATTENTION_LANES), doc_ids, doc_before))
    return outputs.reshape(STACKED_SPOTS, D_MODEL)
```

```python
import functools

import jax
import jax.numpy as jnp
from jax import lax
from jax.experimental import pallas as pl
from jax.experimental.pallas import tpu as pltpu
from jax.sharding import PartitionSpec as P

ATTENTION_LANES = 48
HEAD_DIM = 64
NORM_EPS = 1e-05
LANES = 128
F32 = jnp.float32
BF16 = jnp.bfloat16
MESH = pl.DeviceIdType.MESH


def iota(shape, axis):
    return lax.broadcasted_iota(jnp.int32, shape, axis)


def dot(a, b):
    return jnp.dot(a, b, preferred_element_type=F32)


def dot_nt(a, b):
    return lax.dot_general(a, b, (((1,), (1,)), ((), ())), preferred_element_type=F32)


def layer_kernel(
    n,
    steps,
    heads,
    docs,
    target_ref,
    doc_ref,
    skip_ref,
    x_ref,
    z_ref,
    b_ref,
    c_ref,
    small_ref,
    gain_ref,
    w_ref,
    out_ref,
    send_aux,
    send_x,
    send_z,
    recv_aux,
    recv_x,
    recv_z,
    state_send,
    state_recv,
    xs_ref,
    xw_ref,
    zs_ref,
    cs_ref,
    gm_ref,
    mixed_ref,
    gs_ref,
    sq_ref,
    sq_recv,
    a_send,
    a_recv,
    y_send,
    y_recv,
    out_sem,
    in_sem,
    state_out_sem,
    state_in_sem,
    head_out_sem,
    head_in_sem,
):
    tok, wide = x_ref.shape
    cap = tok // n
    state = b_ref.shape[1]
    pairs = wide // LANES
    half = tok // 2
    own = tok // 4
    me = lax.axis_index("seq")
    hd = lax.axis_index("head")
    core, side = hd % 2, hd // 2
    core_peer = side * 2 + (1 - core)
    side_peer = (1 - side) * 2 + core

    barrier = pltpu.get_barrier_semaphore()

    def greet(k, carry):
        pl.semaphore_signal(
            barrier, inc=1, device_id={"seq": (me + k) % n}, device_id_type=MESH
        )
        return carry

    lax.fori_loop(1, n, greet, 0)
    for k in range(1, 4):
        pl.semaphore_signal(
            barrier, inc=1, device_id={"head": (hd + k) % 4}, device_id_type=MESH
        )

    target = target_ref[...]
    owner = target // tok
    place = target - owner * tok
    far = (owner - me + n) % n
    groups = max(n, 16)
    hits = (iota((groups, tok), 0) == far).astype(F32)
    before = (iota((tok, tok), 0) < iota((tok, tok), 1)).astype(F32).astype(BF16)
    rank = jnp.sum(dot(hits.astype(BF16), before) * hits, axis=0, keepdims=True)
    slot = far * cap + rank.astype(jnp.int32)
    perm = (iota((tok, tok), 0) == slot).astype(F32).astype(BF16)
    high = place // 16
    row = iota((LANES, tok), 0)
    small_t = jnp.where(
        row == heads,
        high.astype(F32),
        jnp.where(row == heads + 1, (place - high * 16).astype(F32), small_ref[...].astype(F32)),
    ).astype(BF16)

    def copy_of(which, send, recv, k):
        return pltpu.make_async_remote_copy(
            src_ref=send.at[k],
            dst_ref=recv.at[k],
            send_sem=out_sem.at[which, k],
            recv_sem=in_sem.at[which, k],
            device_id={"seq": (me + k) % n},
            device_id_type=MESH,
        )

    def start_all(which, send, recv, first, last):
        def go(k, carry):
            copy_of(which, send, recv, k).start()
            return carry

        lax.fori_loop(first, last, go, 0)

    def wait_in(which, send, recv):
        def go(k, carry):
            copy_of(which, send, recv, k).wait_recv()
            return carry

        lax.fori_loop(1, n, go, 0)

    def wait_out(which, send, recv):
        def go(k, carry):
            copy_of(which, send, recv, k).wait_send()
            return carry

        lax.fori_loop(1, n, go, 0)

    def by_slot(values):
        return values.reshape(values.shape[0] // cap, cap, values.shape[1]).astype(BF16)

    def packed_rows(ref):
        if cap % 16 == 0:
            return ref[...].reshape(tok, ref.shape[2])
        return ref[...].astype(F32).reshape(tok, ref.shape[2]).astype(BF16)

    send_aux[:, :, 0:state] = by_slot(dot(perm, b_ref[...]))
    send_aux[:, :, state : 2 * state] = by_slot(dot(perm, c_ref[...]))
    send_aux[:, :, 2 * state :] = by_slot(dot_nt(perm, small_t))
    pl.semaphore_wait(barrier, n - 1 + 3)
    start_all(0, send_aux, recv_aux, 1, n)
    recv_aux[0] = send_aux[0]
    for part in range(2):
        lo, hi = part * n // 2, (part + 1) * n // 2
        send_x[lo:hi] = by_slot(dot(perm[lo * cap : hi * cap], x_ref[...]))
        start_all(1, send_x, recv_x, max(lo, 1), hi)
    recv_x[0] = send_x[0]
    send_z[...] = by_slot(dot(perm, z_ref[...]))
    start_all(2, send_z, recv_z, 1, n)
    recv_z[0] = send_z[0]

    first_place = me * tok
    col = iota((tok, 1), 0)
    line = iota((1, tok), 1)
    doc_col = jnp.zeros((tok, 1), jnp.int32)
    doc_line = jnp.zeros((1, tok), jnp.int32)
    doc_last = jnp.int32(0)
    doc_before = jnp.int32(0)
    start = jnp.int32(0)
    for k in range(docs):
        doc_col += jnp.where(col + first_place >= start, 1, 0)
        doc_line += jnp.where(line + first_place >= start, 1, 0)
        doc_last += jnp.where(first_place + tok - 1 >= start, 1, 0)
        doc_before += jnp.where(first_place - 1 >= start, 1, 0)
        start = start + doc_ref[k]
    low = iota((tok, tok), 0) >= iota((tok, tok), 1)
    lane = iota((1, LANES), 1)
    left = lane < HEAD_DIM

    wait_in(0, send_aux, recv_aux)
    aux = packed_rows(recv_aux)
    small_back = aux[:, 2 * state :].astype(F32).T
    places = small_back[heads : heads + 1] * 16.0 + small_back[heads + 1 : heads + 2]
    unperm = (iota((tok, tok), 0) == places.astype(jnp.int32)).astype(F32).astype(BF16)
    aux = dot(unperm, aux)
    b_t = aux[:, 0:state].T.astype(BF16)
    cs_ref[...] = aux[:, state : 2 * state].astype(BF16)
    decays = jnp.where(lane < heads, aux[:, 2 * state :], 0.0).astype(BF16)
    running = dot(low.astype(F32).astype(BF16), decays)
    running_t = running.T
    closing = running[tok - 1 : tok]
    weight = jnp.exp(closing - running) * jnp.where(doc_col == doc_last, 1.0, 0.0)
    entry = jnp.exp(running) * jnp.where(doc_col == doc_before, 1.0, 0.0)
    through = jnp.exp(closing) * jnp.where(doc_last == doc_before, 1.0, 0.0)
    allowed = low & (doc_col == doc_line)
    gm_ref[...] = jnp.where(allowed, dot(cs_ref[...], b_t), 0.0)

    def spread(values, j):
        return jnp.where(left, values[:, 2 * j : 2 * j + 1], values[:, 2 * j + 1 : 2 * j + 2])

    wait_in(1, send_x, recv_x)
    xs_ref[...] = dot(unperm, packed_rows(recv_x)).astype(BF16)
    for j in range(pairs):
        cols = slice(j * LANES, (j + 1) * LANES)
        xw_ref[:, cols] = (xs_ref[:, cols].astype(F32) * spread(weight, j)).astype(BF16)
    held = dot(b_t, xw_ref[...])
    kept = jnp.concatenate([spread(through, j) for j in range(pairs)], axis=1)

    def state_copy(step):
        gap = 1 if step == 0 else 2 ** (step - 1)
        copy = pltpu.make_async_remote_copy(
            src_ref=state_send.at[step],
            dst_ref=state_recv.at[step],
            send_sem=state_out_sem.at[step],
            recv_sem=state_in_sem.at[step],
            device_id={"seq": (me + gap) % n},
            device_id_type=MESH,
        )
        return copy, gap

    def state_start(step, held, kept):
        state_send[step, 0:state] = held.astype(BF16)
        upper = kept.astype(BF16).astype(F32)
        rows = iota((16, wide), 0)
        state_send[step, state:] = jnp.where(
            rows == 0, upper, jnp.where(rows == 1, kept - upper, 0.0)
        ).astype(BF16)
        copy, gap = state_copy(step)

        @pl.when(me + gap < n)
        def _():
            copy.start()

    def state_finish(step, held, kept):
        copy, gap = state_copy(step)

        @pl.when(me >= gap)
        def _():
            copy.wait_recv()

        @pl.when(me < gap)
        def _():
            state_recv[step] = jnp.zeros(state_recv.shape[1:], BF16)

        came = state_recv[step, 0:state].astype(F32)
        tail = state_recv[step, state:].astype(F32)
        came_kept = tail[0:1] + tail[1:2]
        if step == 0:
            return came, came_kept
        return held + kept * came, kept * came_kept

    def inner(j):
        cols = slice(j * LANES, (j + 1) * LANES)
        skip = jnp.where(left, skip_ref[2 * j], skip_ref[2 * j + 1])
        for t0 in range(0, tok, half):
            rows = slice(t0, t0 + half)
            upto = t0 + half
            keys = xs_ref[0:upto, cols]
            sums = []
            for h in (2 * j, 2 * j + 1):
                gaps = jnp.minimum(
                    running[rows, h : h + 1] - running_t[h : h + 1, 0:upto], 0.0
                )
                scores = (gm_ref[rows, 0:upto] * jnp.exp(gaps)).astype(BF16)
                sums.append(dot(scores, keys))
            mixed_ref[rows, cols] = (
                jnp.where(left, sums[0], sums[1]) + skip * xs_ref[rows, cols].astype(F32)
            )

    state_start(0, held, kept)
    done = 0
    for step in range(steps):
        until = pairs * (step + 1) // steps
        for j in range(done, until):
            inner(j)
        done = until
        if step == steps - 1:
            wait_in(2, send_z, recv_z)
            zs_ref[...] = dot(unperm, packed_rows(recv_z)).astype(BF16)
        held, kept = state_finish(step, held, kept)
        if step + 1 < steps:
            state_start(step + 1, held, kept)
    entry_state = held.astype(BF16)
    mixed_ref[...] += dot(cs_ref[...], entry_state) * jnp.concatenate(
        [spread(entry, j) for j in range(pairs)], axis=1
    )

    def gate_half(where):
        rows = pl.ds(pl.multiple_of(where * half, half), half)
        gate = zs_ref[rows, :].astype(F32)
        gated = mixed_ref[rows, :] * (gate / (1.0 + jnp.exp(-gate)))
        gs_ref[rows, :] = (gated * gain_ref[...]).astype(BF16)
        squares = jnp.sum(gated * gated, axis=1, keepdims=True)
        squares = jnp.broadcast_to(squares, (half, LANES)).T[0:8]
        for i in range(2):
            sq_ref[pl.ds(2 * where + i, 1)] = squares[None, :, i * own : (i + 1) * own]

    def partial(where_side, where_core):
        at = (where_side * 2 + where_core) * own
        return dot(gs_ref[pl.ds(pl.multiple_of(at, own), own), :], w_ref[...])

    def head_copy(which, src, dst, peer):
        return pltpu.make_async_remote_copy(
            src_ref=src,
            dst_ref=dst,
            send_sem=head_out_sem.at[which],
            recv_sem=head_in_sem.at[which],
            device_id={"head": peer},
            device_id_type=MESH,
        )

    copies = [head_copy(i, a_send.at[i], a_recv.at[i], core_peer) for i in range(2)]
    across = head_copy(2, y_send, y_recv, side_peer)
    gate_half(1 - side)
    a_send[0] = partial(1 - side, 1 - core).astype(BF16)
    copies[0].start()
    passing = partial(1 - side, core)
    copies[0].wait_recv()
    y_send[...] = (passing + a_recv[0].astype(F32)).astype(BF16)
    across.start()
    gate_half(side)
    sq_copies = [
        head_copy(2 + k, sq_ref.at[(hd + k) % 4], sq_recv.at[k], (hd + k) % 4) for k in range(1, 4)
    ]
    for copy in sq_copies:
        copy.start()
    a_send[1] = partial(side, 1 - core).astype(BF16)
    copies[1].start()
    total = partial(side, core)
    for copy in sq_copies:
        copy.wait_recv()
    squares = sq_ref[pl.ds(hd, 1)][0] + sq_recv[1] + sq_recv[2] + sq_recv[3]
    scale = lax.rsqrt(squares / (ATTENTION_LANES * HEAD_DIM) + NORM_EPS)
    scale = jnp.broadcast_to(scale[0:1], (LANES, own)).T[:, 0:1]
    copies[1].wait_recv()
    total = total + a_recv[1].astype(F32)
    across.wait_recv()
    out_ref[...] = ((total + y_recv[...].astype(F32)) * scale).astype(BF16)

    wait_out(0, send_aux, recv_aux)
    wait_out(1, send_x, recv_x)
    wait_out(2, send_z, recv_z)
    for step in range(steps):
        copy, gap = state_copy(step)

        @pl.when(me + gap < n)
        def _():
            copy.wait_send()

    for copy in copies + [across] + sq_copies:
        copy.wait_send()


def body(
    features_in,
    gate_in,
    b_input,
    c_input,
    log_decay,
    row_target,
    doc_lengths,
    skip_gain,
    norm_gain,
    out_weight,
):
    tok, wide = features_in.shape
    heads = log_decay.shape[1]
    state = b_input.shape[1]
    model = out_weight.shape[1]
    n = lax.axis_size("seq")
    cap = tok // n
    aux = 2 * state + LANES
    steps, reach = 1, 1
    while reach < n // 2:
        steps, reach = steps + 1, reach * 2
    small = jnp.pad(log_decay.T, ((0, LANES - heads), (0, 0)))
    vmem = pl.BlockSpec(memory_space=pltpu.VMEM)
    smem = pl.BlockSpec(memory_space=pltpu.SMEM)
    own = tok // 4
    kernel = functools.partial(layer_kernel, n, steps, heads, doc_lengths.shape[0])
    return pl.pallas_call(
        kernel,
        out_shape=jax.ShapeDtypeStruct((own, model), BF16),
        in_specs=[vmem, smem, smem] + [vmem] * 7,
        out_specs=vmem,
        scratch_shapes=[
            pltpu.VMEM((n, cap, aux), BF16),
            pltpu.VMEM((n, cap, wide), BF16),
            pltpu.VMEM((n, cap, wide), BF16),
            pltpu.VMEM((n, cap, aux), BF16),
            pltpu.VMEM((n, cap, wide), BF16),
            pltpu.VMEM((n, cap, wide), BF16),
            pltpu.VMEM((steps, state + 16, wide), BF16),
            pltpu.VMEM((steps, state + 16, wide), BF16),
            pltpu.VMEM((tok, wide), BF16),
            pltpu.VMEM((tok, wide), BF16),
            pltpu.VMEM((tok, wide), BF16),
            pltpu.VMEM((tok, state), BF16),
            pltpu.VMEM((tok, tok), F32),
            pltpu.VMEM((tok, wide), F32),
            pltpu.VMEM((tok, wide), BF16),
            pltpu.VMEM((4, 8, own), F32),
            pltpu.VMEM((4, 8, own), F32),
            pltpu.VMEM((2, own, model), BF16),
            pltpu.VMEM((2, own, model), BF16),
            pltpu.VMEM((own, model), BF16),
            pltpu.VMEM((own, model), BF16),
            pltpu.SemaphoreType.DMA((3, n)),
            pltpu.SemaphoreType.DMA((3, n)),
            pltpu.SemaphoreType.DMA((steps,)),
            pltpu.SemaphoreType.DMA((steps,)),
            pltpu.SemaphoreType.DMA((6,)),
            pltpu.SemaphoreType.DMA((6,)),
        ],
        compiler_params=pltpu.CompilerParams(
            collective_id=0, has_side_effects=True, vmem_limit_bytes=52 * 1024 * 1024
        ),
        name="layer",
    )(
        row_target.reshape(1, tok),
        doc_lengths,
        skip_gain,
        features_in,
        gate_in,
        b_input,
        c_input,
        small,
        norm_gain.reshape(1, wide),
        out_weight,
    )


def solution(mesh):
    in_specs = (
        P("seq", "head"),
        P("seq", "head"),
        P("seq", None),
        P("seq", None),
        P("seq", "head"),
        P("seq"),
        P(),
        P("head"),
        P("head"),
        P("head", None),
    )
    out_specs = P(("seq", "head"), None)
    return jax.shard_map(body, mesh=mesh, in_specs=in_specs, out_specs=out_specs, check_vma=False)
```

```python
import functools

import jax
import jax.numpy as jnp
from jax import lax
from jax.experimental import pallas as pl
from jax.experimental.pallas import tpu as pltpu
from jax.sharding import PartitionSpec as P

ATTENTION_LANES = 48
HEAD_DIM = 64
NORM_EPS = 1e-05
LANES = 128
F32 = jnp.float32
BF16 = jnp.bfloat16
MESH = pl.DeviceIdType.MESH


def iota(shape, axis):
    return lax.broadcasted_iota(jnp.int32, shape, axis)


def dot(a, b):
    return jnp.dot(a, b, preferred_element_type=F32)


def dot_nt(a, b):
    return lax.dot_general(a, b, (((1,), (1,)), ((), ())), preferred_element_type=F32)


def layer_kernel(
    n,
    gaps,
    heads,
    docs,
    target_ref,
    doc_ref,
    skip_ref,
    x_hbm,
    z_hbm,
    b_hbm,
    c_hbm,
    small_ref,
    gain_ref,
    w_hbm,
    out_ref,
    x_ref,
    z_ref,
    b_ref,
    c_ref,
    w_ref,
    small_f,
    load_sem,
    send_bc,
    recv_bc,
    bc_out_sem,
    bc_in_sem,
    share_sem,
    send_aux,
    send_x,
    send_z,
    recv_aux,
    recv_x,
    recv_z,
    pair_send,
    pair_recv,
    state_send,
    state_recv,
    last_send,
    last_recv,
    xs_ref,
    xw_ref,
    zs_ref,
    cs_ref,
    gm_ref,
    mixed_ref,
    gs_ref,
    sq_ref,
    sq_recv,
    a_send,
    a_recv,
    y_send,
    y_recv,
    out_sem,
    in_sem,
    state_out_sem,
    state_in_sem,
    head_out_sem,
    head_in_sem,
):
    tok, wide = x_ref.shape
    cap = tok // n
    state = b_ref.shape[1]
    pairs = wide // LANES
    half = tok // 2
    own = tok // 4
    me = lax.axis_index("seq")
    hd = lax.axis_index("head")
    core, side = hd % 2, hd // 2
    core_peer = side * 2 + (1 - core)
    side_peer = (1 - side) * 2 + core

    column = me % 2
    pair_peer = me + 1 - 2 * column
    loads = [
        pltpu.make_async_copy(src, dst, load_sem.at[i])
        for i, (src, dst) in enumerate(
            (
                (b_hbm, b_ref),
                (c_hbm, c_ref),
                (x_hbm, x_ref),
                (z_hbm, z_ref),
                (w_hbm, w_ref),
            )
        )
    ]
    for load in loads:
        load.start()

    barrier = pltpu.get_barrier_semaphore()

    def greet(k, carry):
        pl.semaphore_signal(
            barrier, inc=1, device_id={"seq": (me + k) % n}, device_id_type=MESH
        )
        return carry

    lax.fori_loop(1, n, greet, 0)
    for k in range(1, 4):
        pl.semaphore_signal(
            barrier, inc=1, device_id={"head": (hd + k) % 4}, device_id_type=MESH
        )

    target = target_ref[...]
    owner = target // tok
    place = target - owner * tok
    far = (owner - me + n) % n
    groups = max(n, 16)
    hits = (iota((groups, tok), 0) == far).astype(F32)
    before = (iota((tok, tok), 0) < iota((tok, tok), 1)).astype(F32).astype(BF16)
    rank = jnp.sum(dot(hits.astype(BF16), before) * hits, axis=0, keepdims=True)
    slot = far * cap + rank.astype(jnp.int32)
    perm = (iota((tok, tok), 0) == slot).astype(F32).astype(BF16)
    high = place // 16
    small_f[...] = jnp.zeros_like(small_f)
    small_f[0:heads] = small_ref[...].astype(F32)
    small_f[heads : heads + 1] = high.astype(F32)
    small_f[heads + 1 : heads + 2] = (place - high * 16).astype(F32)
    small_t = small_f[...].astype(BF16)

    def copy_of(which, send, recv, k):
        return pltpu.make_async_remote_copy(
            src_ref=send.at[k],
            dst_ref=recv.at[k],
            send_sem=out_sem.at[which, k],
            recv_sem=in_sem.at[which, k],
            device_id={"seq": (me + k) % n},
            device_id_type=MESH,
        )

    def start_all(which, send, recv, first, last):
        def go(k, carry):
            copy_of(which, send, recv, k).start()
            return carry

        lax.fori_loop(first, last, go, 0)

    def wait_in(which, send, recv):
        def go(k, carry):
            copy_of(which, send, recv, k).wait_recv()
            return carry

        lax.fori_loop(1, n, go, 0)

    def wait_out(which, send, recv):
        def go(k, carry):
            copy_of(which, send, recv, k).wait_send()
            return carry

        lax.fori_loop(1, n, go, 0)

    def by_slot(values):
        return values.reshape(values.shape[0] // cap, cap, values.shape[1]).astype(BF16)

    def packed_rows(ref):
        if cap % 16 == 0:
            return ref[...].reshape(tok, ref.shape[2])
        return ref[...].astype(F32).reshape(tok, ref.shape[2]).astype(BF16)

    def bc_copy(k):
        return pltpu.make_async_remote_copy(
            src_ref=send_bc.at[k],
            dst_ref=recv_bc.at[k],
            send_sem=bc_out_sem.at[k],
            recv_sem=bc_in_sem.at[k],
            device_id={"seq": (me + k) % n},
            device_id_type=MESH,
        )

    def bc_share(i, p):
        k = hd + 4 * i
        return pltpu.make_async_remote_copy(
            src_ref=recv_bc.at[k],
            dst_ref=recv_bc.at[k],
            send_sem=share_sem.at[i, p],
            recv_sem=bc_in_sem.at[k],
            device_id={"head": (hd + p) % 4},
            device_id_type=MESH,
        )

    def mine(act):
        def go(i, carry):
            @pl.when(hd + 4 * i >= 1)
            def _():
                act(i, hd + 4 * i)

            return carry

        lax.fori_loop(0, n // 4, go, 0)

    loads[0].wait()
    loads[1].wait()
    send_bc[:, :, 0:state] = by_slot(dot(perm, b_ref[...]))
    send_bc[:, :, state:] = by_slot(dot(perm, c_ref[...]))
    send_aux[...] = by_slot(dot_nt(perm, small_t))
    pl.semaphore_wait(barrier, n - 1 + 3)
    mine(lambda i, k: bc_copy(k).start())
    start_all(0, send_aux, recv_aux, 1, n)
    recv_aux[0] = send_aux[0]
    recv_bc[0] = send_bc[0]
    loads[2].wait()
    for part in range(2):
        lo, hi = part * n // 2, (part + 1) * n // 2
        send_x[lo:hi] = by_slot(dot(perm[lo * cap : hi * cap], x_ref[...]))
        start_all(1, send_x, recv_x, max(lo, 1), hi)
    recv_x[0] = send_x[0]
    loads[3].wait()
    send_z[...] = by_slot(dot(perm, z_ref[...]))
    start_all(2, send_z, recv_z, 1, n)
    recv_z[0] = send_z[0]

    first_place = me * tok
    col = iota((tok, 1), 0)
    line = iota((1, tok), 1)
    doc_col = jnp.zeros((tok, 1), jnp.int32)
    doc_line = jnp.zeros((1, tok), jnp.int32)
    doc_last = jnp.int32(0)
    doc_before = jnp.int32(0)
    start = jnp.int32(0)
    for k in range(docs):
        doc_col += jnp.where(col + first_place >= start, 1, 0)
        doc_line += jnp.where(line + first_place >= start, 1, 0)
        doc_last += jnp.where(first_place + tok - 1 >= start, 1, 0)
        doc_before += jnp.where(first_place - 1 >= start, 1, 0)
        start = start + doc_ref[k]
    low = iota((tok, tok), 0) >= iota((tok, tok), 1)
    lane = iota((1, LANES), 1)
    left = lane < HEAD_DIM

    def share(i, k):
        bc_copy(k).wait_recv()
        for p in range(1, 4):
            bc_share(i, p).start()

    mine(share)
    wait_in(0, send_aux, recv_aux)
    aux = packed_rows(recv_aux)
    small_back = aux.astype(F32).T
    places = small_back[heads : heads + 1] * 16.0 + small_back[heads + 1 : heads + 2]
    unperm = (iota((tok, tok), 0) == places.astype(jnp.int32)).astype(F32).astype(BF16)
    aux = dot(unperm, aux)

    def shared(k, carry):
        @pl.when(k % 4 != hd)
        def _():
            bc_copy(k).wait_recv()

        return carry

    lax.fori_loop(1, n, shared, 0)
    both = dot(unperm, packed_rows(recv_bc))
    b_t = both[:, 0:state].T.astype(BF16)
    cs_ref[...] = both[:, state:].astype(BF16)
    decays = jnp.where(lane < heads, aux, 0.0).astype(BF16)
    running = dot(low.astype(F32).astype(BF16), decays)
    running_t = running.T
    closing = running[tok - 1 : tok]
    weight = jnp.exp(closing - running) * jnp.where(doc_col == doc_last, 1.0, 0.0)
    entry = jnp.exp(running) * jnp.where(doc_col == doc_before, 1.0, 0.0)
    through = jnp.exp(closing) * jnp.where(doc_last == doc_before, 1.0, 0.0)
    allowed = low & (doc_col == doc_line)
    gm_ref[...] = jnp.where(allowed, dot(cs_ref[...], b_t), 0.0)

    def spread(values, j):
        return jnp.where(left, values[:, 2 * j : 2 * j + 1], values[:, 2 * j + 1 : 2 * j + 2])

    wait_in(1, send_x, recv_x)
    xs_ref[...] = dot(unperm, packed_rows(recv_x)).astype(BF16)
    for j in range(pairs):
        cols = slice(j * LANES, (j + 1) * LANES)
        xw_ref[:, cols] = (xs_ref[:, cols].astype(F32) * spread(weight, j)).astype(BF16)
    held = dot(b_t, xw_ref[...])
    kept = jnp.concatenate([spread(through, j) for j in range(pairs)], axis=1)

    def fill(ref, held, kept):
        ref[0:state] = held.astype(BF16)
        upper = kept.astype(BF16).astype(F32)
        rows = iota((16, kept.shape[1]), 0)
        ref[state:] = jnp.where(
            rows == 0, upper, jnp.where(rows == 1, kept - upper, 0.0)
        ).astype(BF16)

    def read(ref):
        tail = ref[state:].astype(F32)
        return ref[0:state].astype(F32), tail[0:1] + tail[1:2]

    def pair_copy(which, src, dst):
        return pltpu.make_async_remote_copy(
            src_ref=src,
            dst_ref=dst,
            send_sem=state_out_sem.at[which],
            recv_sem=state_in_sem.at[which],
            device_id={"seq": pair_peer},
            device_id_type=MESH,
        )

    def state_copy(step):
        return pltpu.make_async_remote_copy(
            src_ref=state_send.at[step],
            dst_ref=state_recv.at[step],
            send_sem=state_out_sem.at[2 + step],
            recv_sem=state_in_sem.at[2 + step],
            device_id={"seq": (me + 2 * gaps[step]) % n},
            device_id_type=MESH,
        )

    def state_start(step, held, kept):
        fill(state_send.at[step], held, kept)

        @pl.when(me + 2 * gaps[step] < n)
        def _():
            state_copy(step).start()

    def state_finish(step):
        @pl.when(me >= 2 * gaps[step])
        def _():
            state_copy(step).wait_recv()

        @pl.when(me < 2 * gaps[step])
        def _():
            state_recv[step] = jnp.zeros(state_recv.shape[1:], BF16)

        return read(state_recv.at[step])

    def inner(j):
        cols = slice(j * LANES, (j + 1) * LANES)
        skip = jnp.where(left, skip_ref[2 * j], skip_ref[2 * j + 1])
        for t0 in range(0, tok, half):
            rows = slice(t0, t0 + half)
            upto = t0 + half
            keys = xs_ref[0:upto, cols]
            sums = []
            for h in (2 * j, 2 * j + 1):
                gaps = jnp.minimum(
                    running[rows, h : h + 1] - running_t[h : h + 1, 0:upto], 0.0
                )
                scores = (gm_ref[rows, 0:upto] * jnp.exp(gaps)).astype(BF16)
                sums.append(dot(scores, keys))
            mixed_ref[rows, cols] = (
                jnp.where(left, sums[0], sums[1]) + skip * xs_ref[rows, cols].astype(F32)
            )

    stages = len(gaps) + 2

    def inner_of(stage):
        for j in range(pairs * stage // stages, pairs * (stage + 1) // stages):
            inner(j)

    first_copy = pair_copy(0, pair_send, pair_recv)
    last_copy = pair_copy(1, last_send, last_recv)
    fill(pair_send, held, kept)
    first_copy.start()
    inner_of(0)
    first_copy.wait_recv()
    part = wide // 2
    other, other_kept = read(pair_recv)

    def ordered(own_one, other_one):
        early = jnp.where(column == 0, own_one, other_one)
        late = jnp.where(column == 0, other_one, own_one)
        return early, late

    def my_half(values):
        return jnp.where(column == 0, values[:, 0:part], values[:, part:])

    early, late = ordered(my_half(held), my_half(other))
    early_kept, late_kept = ordered(my_half(kept), my_half(other_kept))
    sent, sent_kept = late + late_kept * early, late_kept * early_kept
    for step in range(len(gaps)):
        state_start(step, sent, sent_kept)
        inner_of(1 + step)
        came, came_kept = state_finish(step)
        if step > 0:
            came, came_kept = sent + sent_kept * came, sent_kept * came_kept
        sent, sent_kept = came, came_kept
    last_send[...] = sent.astype(BF16)
    last_copy.start()
    inner_of(stages - 1)
    wait_in(2, send_z, recv_z)
    zs_ref[...] = dot(unperm, packed_rows(recv_z)).astype(BF16)
    last_copy.wait_recv()
    early, late = ordered(last_send[...].astype(F32), last_recv[...].astype(F32))
    held = jnp.concatenate([early, late], axis=1)
    other, other_kept = read(pair_recv)
    held = jnp.where(column == 0, held, other + other_kept * held)
    entry_state = held.astype(BF16)
    mixed_ref[...] += dot(cs_ref[...], entry_state) * jnp.concatenate(
        [spread(entry, j) for j in range(pairs)], axis=1
    )

    def gate_half(where):
        rows = pl.ds(pl.multiple_of(where * half, half), half)
        gate = zs_ref[rows, :].astype(F32)
        gated = mixed_ref[rows, :] * (gate / (1.0 + jnp.exp(-gate)))
        gs_ref[rows, :] = (gated * gain_ref[...].reshape(1, wide)).astype(BF16)
        squares = jnp.sum(gated * gated, axis=1, keepdims=True)
        squares = jnp.broadcast_to(squares, (half, LANES)).T[0:8]
        for i in range(2):
            sq_ref[pl.ds(2 * where + i, 1)] = squares[None, :, i * own : (i + 1) * own]

    def partial(where_side, where_core):
        at = (where_side * 2 + where_core) * own
        return dot(gs_ref[pl.ds(pl.multiple_of(at, own), own), :], w_ref[...])

    def head_copy(which, src, dst, peer):
        return pltpu.make_async_remote_copy(
            src_ref=src,
            dst_ref=dst,
            send_sem=head_out_sem.at[which],
            recv_sem=head_in_sem.at[which],
            device_id={"head": peer},
            device_id_type=MESH,
        )

    loads[4].wait()
    copies = [head_copy(i, a_send.at[i], a_recv.at[i], core_peer) for i in range(2)]
    across = head_copy(2, y_send, y_recv, side_peer)
    gate_half(1 - side)
    a_send[0] = partial(1 - side, 1 - core).astype(BF16)
    copies[0].start()
    passing = partial(1 - side, core)
    copies[0].wait_recv()
    y_send[...] = (passing + a_recv[0].astype(F32)).astype(BF16)
    across.start()
    gate_half(side)
    sq_copies = [
        head_copy(2 + k, sq_ref.at[(hd + k) % 4], sq_recv.at[k], (hd + k) % 4) for k in range(1, 4)
    ]
    for copy in sq_copies:
        copy.start()
    a_send[1] = partial(side, 1 - core).astype(BF16)
    copies[1].start()
    total = partial(side, core)
    for copy in sq_copies:
        copy.wait_recv()
    squares = sq_ref[pl.ds(hd, 1)][0] + sq_recv[1] + sq_recv[2] + sq_recv[3]
    scale = lax.rsqrt(squares / (ATTENTION_LANES * HEAD_DIM) + NORM_EPS)
    scale = jnp.broadcast_to(scale[0:1], (LANES, own)).T[:, 0:1]
    copies[1].wait_recv()
    total = total + a_recv[1].astype(F32)
    across.wait_recv()
    out_ref[...] = ((total + y_recv[...].astype(F32)) * scale).astype(BF16)

    wait_out(0, send_aux, recv_aux)
    wait_out(1, send_x, recv_x)
    wait_out(2, send_z, recv_z)
    mine(lambda i, k: bc_copy(k).wait_send())

    def shared_out(i, k):
        for p in range(1, 4):
            bc_share(i, p).wait_send()

    mine(shared_out)
    first_copy.wait_send()
    last_copy.wait_send()
    for step in range(len(gaps)):

        @pl.when(me + 2 * gaps[step] < n)
        def _():
            state_copy(step).wait_send()

    for copy in copies + [across] + sq_copies:
        copy.wait_send()


def body(
    features_in,
    gate_in,
    b_input,
    c_input,
    log_decay,
    row_target,
    doc_lengths,
    skip_gain,
    norm_gain,
    out_weight,
):
    tok, wide = features_in.shape
    heads = log_decay.shape[1]
    state = b_input.shape[1]
    model = out_weight.shape[1]
    n = lax.axis_size("seq")
    cap = tok // n
    aux = LANES
    gaps, reach = [1], 1
    while reach < n // 4:
        gaps, reach = gaps + [reach], reach * 2
    steps = len(gaps)
    vmem = pl.BlockSpec(memory_space=pltpu.VMEM)
    smem = pl.BlockSpec(memory_space=pltpu.SMEM)
    hbm = pl.BlockSpec(memory_space=pltpu.HBM)
    own = tok // 4
    kernel = functools.partial(layer_kernel, n, gaps, heads, doc_lengths.shape[0])
    return pl.pallas_call(
        kernel,
        out_shape=jax.ShapeDtypeStruct((own, model), BF16),
        in_specs=[vmem, smem, smem] + [hbm] * 4 + [vmem] * 2 + [hbm],
        out_specs=vmem,
        scratch_shapes=[
            pltpu.VMEM((tok, wide), BF16),
            pltpu.VMEM((tok, wide), BF16),
            pltpu.VMEM((tok, state), BF16),
            pltpu.VMEM((tok, state), BF16),
            pltpu.VMEM((wide, model), BF16),
            pltpu.VMEM((LANES, tok), F32),
            pltpu.SemaphoreType.DMA((5,)),
            pltpu.VMEM((n, cap, 2 * state), BF16),
            pltpu.VMEM((n, cap, 2 * state), BF16),
            pltpu.SemaphoreType.DMA((n,)),
            pltpu.SemaphoreType.DMA((n,)),
            pltpu.SemaphoreType.DMA((n // 4, 4)),
            pltpu.VMEM((n, cap, aux), BF16),
            pltpu.VMEM((n, cap, wide), BF16),
            pltpu.VMEM((n, cap, wide), BF16),
            pltpu.VMEM((n, cap, aux), BF16),
            pltpu.VMEM((n, cap, wide), BF16),
            pltpu.VMEM((n, cap, wide), BF16),
            pltpu.VMEM((state + 16, wide), BF16),
            pltpu.VMEM((state + 16, wide), BF16),
            pltpu.VMEM((steps, state + 16, wide // 2), BF16),
            pltpu.VMEM((steps, state + 16, wide // 2), BF16),
            pltpu.VMEM((state, wide // 2), BF16),
            pltpu.VMEM((state, wide // 2), BF16),
            pltpu.VMEM((tok, wide), BF16),
            pltpu.VMEM((tok, wide), BF16),
            pltpu.VMEM((tok, wide), BF16),
            pltpu.VMEM((tok, state), BF16),
            pltpu.VMEM((tok, tok), F32),
            pltpu.VMEM((tok, wide), F32),
            pltpu.VMEM((tok, wide), BF16),
            pltpu.VMEM((4, 8, own), F32),
            pltpu.VMEM((4, 8, own), F32),
            pltpu.VMEM((2, own, model), BF16),
            pltpu.VMEM((2, own, model), BF16),
            pltpu.VMEM((own, model), BF16),
            pltpu.VMEM((own, model), BF16),
            pltpu.SemaphoreType.DMA((3, n)),
            pltpu.SemaphoreType.DMA((3, n)),
            pltpu.SemaphoreType.DMA((steps + 2,)),
            pltpu.SemaphoreType.DMA((steps + 2,)),
            pltpu.SemaphoreType.DMA((6,)),
            pltpu.SemaphoreType.DMA((6,)),
        ],
        compiler_params=pltpu.CompilerParams(
            collective_id=0, has_side_effects=True, vmem_limit_bytes=52 * 1024 * 1024
        ),
        name="layer",
    )(
        row_target.reshape(1, tok),
        doc_lengths,
        skip_gain,
        features_in,
        gate_in,
        b_input,
        c_input,
        log_decay.T,
        norm_gain,
        out_weight,
    )


def solution(mesh):
    in_specs = (
        P("seq", "head"),
        P("seq", "head"),
        P("seq", None),
        P("seq", None),
        P("seq", "head"),
        P("seq"),
        P(),
        P("head"),
        P("head"),
        P("head", None),
    )
    out_specs = P(("seq", "head"), None)
    return jax.shard_map(body, mesh=mesh, in_specs=in_specs, out_specs=out_specs, check_vma=False)
```

```python
import functools

import jax
import jax.numpy as jnp
from jax import lax
from jax.experimental import pallas as pl
from jax.experimental.pallas import tpu as pltpu
from jax.sharding import PartitionSpec as P

ATTENTION_LANES = 48
HEAD_DIM = 64
NORM_EPS = 1e-05
LANES = 128
F32 = jnp.float32
BF16 = jnp.bfloat16
MESH = pl.DeviceIdType.MESH


def iota(shape, axis):
    return lax.broadcasted_iota(jnp.int32, shape, axis)


def dot(a, b):
    return jnp.dot(a, b, preferred_element_type=F32)


def dot_nt(a, b):
    return lax.dot_general(a, b, (((1,), (1,)), ((), ())), preferred_element_type=F32)


def layer_kernel(
    n,
    gaps,
    heads,
    docs,
    target_ref,
    doc_ref,
    skip_ref,
    x_hbm,
    z_hbm,
    b_hbm,
    c_hbm,
    small_ref,
    gain_ref,
    w_hbm,
    out_ref,
    x_ref,
    z_ref,
    b_ref,
    c_ref,
    w_ref,
    small_f,
    load_sem,
    send_bc,
    recv_bc,
    bc_out_sem,
    bc_in_sem,
    share_sem,
    send_aux,
    send_x,
    send_z,
    recv_aux,
    recv_x,
    recv_z,
    pair_send,
    pair_recv,
    state_send,
    state_recv,
    last_send,
    last_recv,
    entry_ref,
    opening_ref,
    xs_ref,
    xw_ref,
    zs_ref,
    cs_ref,
    gm_ref,
    mixed_ref,
    gs_ref,
    sq_ref,
    sq_recv,
    a_send,
    a_recv,
    y_send,
    y_recv,
    out_sem,
    in_sem,
    state_out_sem,
    state_in_sem,
    head_out_sem,
    head_in_sem,
):
    tok, wide = x_ref.shape
    cap = tok // n
    state = b_ref.shape[1]
    pairs = wide // LANES
    half = tok // 2
    own = tok // 4
    me = lax.axis_index("seq")
    hd = lax.axis_index("head")
    core, side = hd % 2, hd // 2
    core_peer = side * 2 + (1 - core)
    side_peer = (1 - side) * 2 + core

    column = me % 2
    pair_peer = me + 1 - 2 * column
    loads = [
        pltpu.make_async_copy(src, dst, load_sem.at[i])
        for i, (src, dst) in enumerate(
            (
                (b_hbm, b_ref),
                (c_hbm, c_ref),
                (x_hbm, x_ref),
                (z_hbm, z_ref),
                (w_hbm, w_ref),
            )
        )
    ]
    for load in loads:
        load.start()

    barrier = pltpu.get_barrier_semaphore()

    def greet(k, carry):
        pl.semaphore_signal(
            barrier, inc=1, device_id={"seq": (me + k) % n}, device_id_type=MESH
        )
        return carry

    lax.fori_loop(1, n, greet, 0)
    for k in range(1, 4):
        pl.semaphore_signal(
            barrier, inc=1, device_id={"head": (hd + k) % 4}, device_id_type=MESH
        )

    target = target_ref[...]
    owner = target // tok
    place = target - owner * tok
    far = (owner - me + n) % n
    groups = max(n, 16)
    hits = (iota((groups, tok), 0) == far).astype(F32)
    before = (iota((tok, tok), 0) < iota((tok, tok), 1)).astype(F32).astype(BF16)
    rank = jnp.sum(dot(hits.astype(BF16), before) * hits, axis=0, keepdims=True)
    slot = far * cap + rank.astype(jnp.int32)
    perm = (iota((tok, tok), 0) == slot).astype(F32).astype(BF16)
    high = place // 16
    small_f[...] = jnp.zeros_like(small_f)
    small_f[0:heads] = small_ref[...].astype(F32)
    small_f[heads : heads + 1] = high.astype(F32)
    small_f[heads + 1 : heads + 2] = (place - high * 16).astype(F32)
    small_t = small_f[...].astype(BF16)

    def copy_of(which, send, recv, k):
        return pltpu.make_async_remote_copy(
            src_ref=send.at[k],
            dst_ref=recv.at[k],
            send_sem=out_sem.at[which, k],
            recv_sem=in_sem.at[which, k],
            device_id={"seq": (me + k) % n},
            device_id_type=MESH,
        )

    def start_all(which, send, recv, first, last):
        def go(k, carry):
            copy_of(which, send, recv, k).start()
            return carry

        lax.fori_loop(first, last, go, 0)

    def wait_in(which, send, recv):
        def go(k, carry):
            copy_of(which, send, recv, k).wait_recv()
            return carry

        lax.fori_loop(1, n, go, 0)

    def wait_out(which, send, recv):
        def go(k, carry):
            copy_of(which, send, recv, k).wait_send()
            return carry

        lax.fori_loop(1, n, go, 0)

    def by_slot(values):
        return values.reshape(values.shape[0] // cap, cap, values.shape[1]).astype(BF16)

    def packed_rows(ref):
        if cap % 16 == 0:
            return ref[...].reshape(tok, ref.shape[2])
        return ref[...].astype(F32).reshape(tok, ref.shape[2]).astype(BF16)

    def bc_copy(k):
        return pltpu.make_async_remote_copy(
            src_ref=send_bc.at[k],
            dst_ref=recv_bc.at[k],
            send_sem=bc_out_sem.at[k],
            recv_sem=bc_in_sem.at[k],
            device_id={"seq": (me + k) % n},
            device_id_type=MESH,
        )

    def bc_share(i, p):
        k = hd + 4 * i
        return pltpu.make_async_remote_copy(
            src_ref=recv_bc.at[k],
            dst_ref=recv_bc.at[k],
            send_sem=share_sem.at[i, p],
            recv_sem=bc_in_sem.at[k],
            device_id={"head": (hd + p) % 4},
            device_id_type=MESH,
        )

    def mine(act):
        def go(i, carry):
            @pl.when(hd + 4 * i >= 1)
            def _():
                act(i, hd + 4 * i)

            return carry

        lax.fori_loop(0, n // 4, go, 0)

    loads[0].wait()
    loads[1].wait()
    send_bc[:, :, 0:state] = by_slot(dot(perm, b_ref[...]))
    send_bc[:, :, state:] = by_slot(dot(perm, c_ref[...]))
    send_aux[...] = by_slot(dot_nt(perm, small_t))
    pl.semaphore_wait(barrier, n - 1 + 3)
    mine(lambda i, k: bc_copy(k).start())
    start_all(0, send_aux, recv_aux, 1, n)
    recv_aux[0] = send_aux[0]
    recv_bc[0] = send_bc[0]
    loads[2].wait()
    for part in range(2):
        lo, hi = part * n // 2, (part + 1) * n // 2
        send_x[lo:hi] = by_slot(dot(perm[lo * cap : hi * cap], x_ref[...]))
        start_all(1, send_x, recv_x, max(lo, 1), hi)
    recv_x[0] = send_x[0]
    loads[3].wait()
    send_z[...] = by_slot(dot(perm, z_ref[...]))
    start_all(2, send_z, recv_z, 1, n)
    recv_z[0] = send_z[0]

    first_place = me * tok
    col = iota((tok, 1), 0)
    line = iota((1, tok), 1)
    doc_col = jnp.zeros((tok, 1), jnp.int32)
    doc_line = jnp.zeros((1, tok), jnp.int32)
    doc_last = jnp.int32(0)
    doc_before = jnp.int32(0)
    start = jnp.int32(0)
    for k in range(docs):
        doc_col += jnp.where(col + first_place >= start, 1, 0)
        doc_line += jnp.where(line + first_place >= start, 1, 0)
        doc_last += jnp.where(first_place + tok - 1 >= start, 1, 0)
        doc_before += jnp.where(first_place - 1 >= start, 1, 0)
        start = start + doc_ref[k]
    low = iota((tok, tok), 0) >= iota((tok, tok), 1)
    lane = iota((1, LANES), 1)
    left = lane < HEAD_DIM

    def share(i, k):
        bc_copy(k).wait_recv()
        for p in range(1, 4):
            bc_share(i, p).start()

    mine(share)
    wait_in(0, send_aux, recv_aux)
    aux = packed_rows(recv_aux)
    small_back = aux.astype(F32).T
    places = small_back[heads : heads + 1] * 16.0 + small_back[heads + 1 : heads + 2]
    unperm = (iota((tok, tok), 0) == places.astype(jnp.int32)).astype(F32).astype(BF16)
    aux = dot(unperm, aux)

    def shared(k, carry):
        @pl.when(k % 4 != hd)
        def _():
            bc_copy(k).wait_recv()

        return carry

    lax.fori_loop(1, n, shared, 0)
    both = dot(unperm, packed_rows(recv_bc))
    b_t = both[:, 0:state].T.astype(BF16)
    cs_ref[...] = both[:, state:].astype(BF16)
    decays = jnp.where(lane < heads, aux, 0.0).astype(BF16)
    running = dot(low.astype(F32).astype(BF16), decays)
    running_t = running.T
    closing = running[tok - 1 : tok]
    weight = jnp.exp(closing - running) * jnp.where(doc_col == doc_last, 1.0, 0.0)
    opening_ref[...] = jnp.exp(running) * jnp.where(doc_col == doc_before, 1.0, 0.0)
    through = jnp.exp(closing) * jnp.where(doc_last == doc_before, 1.0, 0.0)
    allowed = low & (doc_col == doc_line)
    gm_ref[...] = jnp.where(allowed, dot(cs_ref[...], b_t), 0.0)

    def spread(values, j):
        return jnp.where(left, values[:, 2 * j : 2 * j + 1], values[:, 2 * j + 1 : 2 * j + 2])

    wait_in(1, send_x, recv_x)
    xs_ref[...] = dot(unperm, packed_rows(recv_x)).astype(BF16)
    for j in range(pairs):
        cols = slice(j * LANES, (j + 1) * LANES)
        xw_ref[:, cols] = (xs_ref[:, cols].astype(F32) * spread(weight, j)).astype(BF16)
    held = dot(b_t, xw_ref[...])
    kept = jnp.concatenate([spread(through, j) for j in range(pairs)], axis=1)

    def fill(ref, held, kept):
        ref[0:state] = held.astype(BF16)
        upper = kept.astype(BF16).astype(F32)
        rows = iota((16, kept.shape[1]), 0)
        ref[state:] = jnp.where(
            rows == 0, upper, jnp.where(rows == 1, kept - upper, 0.0)
        ).astype(BF16)

    def read(ref):
        tail = ref[state:].astype(F32)
        return ref[0:state].astype(F32), tail[0:1] + tail[1:2]

    def pair_copy(which, src, dst, sem):
        return pltpu.make_async_remote_copy(
            src_ref=src,
            dst_ref=dst,
            send_sem=state_out_sem.at[sem],
            recv_sem=state_in_sem.at[which],
            device_id={"seq": pair_peer},
            device_id_type=MESH,
        )

    def state_copy(step):
        return pltpu.make_async_remote_copy(
            src_ref=state_send.at[step],
            dst_ref=state_recv.at[step],
            send_sem=state_out_sem.at[3 + step],
            recv_sem=state_in_sem.at[3 + step],
            device_id={"seq": (me + 2 * gaps[step]) % n},
            device_id_type=MESH,
        )

    def state_start(step, held, kept):
        fill(state_send.at[step], held, kept)

        @pl.when(me + 2 * gaps[step] < n)
        def _():
            state_copy(step).start()

    def state_finish(step):
        @pl.when(me >= 2 * gaps[step])
        def _():
            state_copy(step).wait_recv()

        @pl.when(me < 2 * gaps[step])
        def _():
            state_recv[step] = jnp.zeros(state_recv.shape[1:], BF16)

        return read(state_recv.at[step])

    def inner(j):
        cols = slice(j * LANES, (j + 1) * LANES)
        skip = jnp.where(left, skip_ref[2 * j], skip_ref[2 * j + 1])
        for t0 in range(0, tok, half):
            rows = slice(t0, t0 + half)
            upto = t0 + half
            keys = xs_ref[0:upto, cols]
            sums = []
            for h in (2 * j, 2 * j + 1):
                gaps = jnp.minimum(
                    running[rows, h : h + 1] - running_t[h : h + 1, 0:upto], 0.0
                )
                scores = (gm_ref[rows, 0:upto] * jnp.exp(gaps)).astype(BF16)
                sums.append(dot(scores, keys))
            mixed_ref[rows, cols] = (
                jnp.where(left, sums[0], sums[1]) + skip * xs_ref[rows, cols].astype(F32)
            )

    stages = len(gaps) + 2

    def inner_of(stage):
        for j in range(pairs * stage // stages, pairs * (stage + 1) // stages):
            inner(j)

    part = wide // 2

    def half_copy(which):
        return pair_copy(which, pair_send.at[which], pair_recv.at[which], which)

    last_copy = pair_copy(2, last_send, last_recv, 2)
    for i in range(2):
        fill(pair_send.at[i], held[:, i * part : (i + 1) * part], kept[:, i * part : (i + 1) * part])
    half_copy(1 - column).start()
    half_copy(column).start()
    inner_of(0)
    half_copy(column).wait_recv()
    other, other_kept = read(pair_recv.at[column])

    def ordered(own_one, other_one):
        early = jnp.where(column == 0, own_one, other_one)
        late = jnp.where(column == 0, other_one, own_one)
        return early, late

    def my_half(values):
        return jnp.where(column == 0, values[:, 0:part], values[:, part:])

    early, late = ordered(my_half(held), other)
    early_kept, late_kept = ordered(my_half(kept), other_kept)
    sent, sent_kept = late + late_kept * early, late_kept * early_kept
    for step in range(len(gaps)):
        state_start(step, sent, sent_kept)
        inner_of(1 + step)
        came, came_kept = state_finish(step)
        if step > 0:
            came, came_kept = sent + sent_kept * came, sent_kept * came_kept
        sent, sent_kept = came, came_kept
    last_send[...] = sent.astype(BF16)
    last_copy.start()
    inner_of(stages - 1)
    wait_in(2, send_z, recv_z)
    gate = dot(unperm, packed_rows(recv_z))
    zs_ref[...] = gate / (1.0 + jnp.exp(-gate))
    last_copy.wait_recv()
    early, late = ordered(last_send[...].astype(F32), last_recv[...].astype(F32))
    half_copy(1 - column).wait_recv()
    for i, came in enumerate((early, late)):
        other, other_kept = read(pair_recv.at[i])
        came = jnp.where(column == 0, came, other + other_kept * came)
        entry_ref[:, i * part : (i + 1) * part] = came.astype(BF16)

    def gate_rows(where_side, where_core):
        at = where_side * 2 + where_core
        rows = pl.ds(pl.multiple_of(at * own, own), own)
        share = opening_ref[rows, :]
        share = jnp.concatenate([spread(share, j) for j in range(pairs)], axis=1)
        gated = mixed_ref[rows, :] + dot(cs_ref[rows, :], entry_ref[...]) * share
        gated = gated * zs_ref[rows, :]
        gs_ref[rows, :] = (gated * gain_ref[...].reshape(1, wide)).astype(BF16)
        squares = jnp.sum(gated * gated, axis=1, keepdims=True)
        squares = jnp.broadcast_to(squares, (own, LANES)).T[0:8]
        sq_ref[pl.ds(at, 1)] = squares[None]

    def partial(where_side, where_core):
        at = (where_side * 2 + where_core) * own
        return dot(gs_ref[pl.ds(pl.multiple_of(at, own), own), :], w_ref[...])

    def head_copy(which, src, dst, peer):
        return pltpu.make_async_remote_copy(
            src_ref=src,
            dst_ref=dst,
            send_sem=head_out_sem.at[which],
            recv_sem=head_in_sem.at[which],
            device_id={"head": peer},
            device_id_type=MESH,
        )

    loads[4].wait()
    copies = [head_copy(i, a_send.at[i], a_recv.at[i], core_peer) for i in range(2)]
    across = head_copy(2, y_send, y_recv, side_peer)
    gate_rows(1 - side, 1 - core)
    a_send[0] = partial(1 - side, 1 - core).astype(BF16)
    copies[0].start()
    gate_rows(1 - side, core)
    passing = partial(1 - side, core)
    copies[0].wait_recv()
    y_send[...] = (passing + a_recv[0].astype(F32)).astype(BF16)
    across.start()
    gate_rows(side, 1 - core)
    a_send[1] = partial(side, 1 - core).astype(BF16)
    copies[1].start()
    gate_rows(side, core)
    sq_copies = [
        head_copy(2 + k, sq_ref.at[(hd + k) % 4], sq_recv.at[k], (hd + k) % 4) for k in range(1, 4)
    ]
    for copy in sq_copies:
        copy.start()
    total = partial(side, core)
    for copy in sq_copies:
        copy.wait_recv()
    squares = sq_ref[pl.ds(hd, 1)][0] + sq_recv[1] + sq_recv[2] + sq_recv[3]
    scale = lax.rsqrt(squares / (ATTENTION_LANES * HEAD_DIM) + NORM_EPS)
    scale = jnp.broadcast_to(scale[0:1], (LANES, own)).T[:, 0:1]
    copies[1].wait_recv()
    total = total + a_recv[1].astype(F32)
    across.wait_recv()
    out_ref[...] = ((total + y_recv[...].astype(F32)) * scale).astype(BF16)

    wait_out(0, send_aux, recv_aux)
    wait_out(1, send_x, recv_x)
    wait_out(2, send_z, recv_z)
    mine(lambda i, k: bc_copy(k).wait_send())

    def shared_out(i, k):
        for p in range(1, 4):
            bc_share(i, p).wait_send()

    mine(shared_out)
    for i in range(2):
        half_copy(i).wait_send()
    last_copy.wait_send()
    for step in range(len(gaps)):

        @pl.when(me + 2 * gaps[step] < n)
        def _():
            state_copy(step).wait_send()

    for copy in copies + [across] + sq_copies:
        copy.wait_send()


def body(
    features_in,
    gate_in,
    b_input,
    c_input,
    log_decay,
    row_target,
    doc_lengths,
    skip_gain,
    norm_gain,
    out_weight,
):
    tok, wide = features_in.shape
    heads = log_decay.shape[1]
    state = b_input.shape[1]
    model = out_weight.shape[1]
    n = lax.axis_size("seq")
    cap = tok // n
    aux = LANES
    gaps, reach = [1], 1
    while reach < n // 4:
        gaps, reach = gaps + [reach], reach * 2
    steps = len(gaps)
    vmem = pl.BlockSpec(memory_space=pltpu.VMEM)
    smem = pl.BlockSpec(memory_space=pltpu.SMEM)
    hbm = pl.BlockSpec(memory_space=pltpu.HBM)
    own = tok // 4
    kernel = functools.partial(layer_kernel, n, gaps, heads, doc_lengths.shape[0])
    return pl.pallas_call(
        kernel,
        out_shape=jax.ShapeDtypeStruct((own, model), BF16),
        in_specs=[vmem, smem, smem] + [hbm] * 4 + [vmem] * 2 + [hbm],
        out_specs=vmem,
        scratch_shapes=[
            pltpu.VMEM((tok, wide), BF16),
            pltpu.VMEM((tok, wide), BF16),
            pltpu.VMEM((tok, state), BF16),
            pltpu.VMEM((tok, state), BF16),
            pltpu.VMEM((wide, model), BF16),
            pltpu.VMEM((LANES, tok), F32),
            pltpu.SemaphoreType.DMA((5,)),
            pltpu.VMEM((n, cap, 2 * state), BF16),
            pltpu.VMEM((n, cap, 2 * state), BF16),
            pltpu.SemaphoreType.DMA((n,)),
            pltpu.SemaphoreType.DMA((n,)),
            pltpu.SemaphoreType.DMA((n // 4, 4)),
            pltpu.VMEM((n, cap, aux), BF16),
            pltpu.VMEM((n, cap, wide), BF16),
            pltpu.VMEM((n, cap, wide), BF16),
            pltpu.VMEM((n, cap, aux), BF16),
            pltpu.VMEM((n, cap, wide), BF16),
            pltpu.VMEM((n, cap, wide), BF16),
            pltpu.VMEM((2, state + 16, wide // 2), BF16),
            pltpu.VMEM((2, state + 16, wide // 2), BF16),
            pltpu.VMEM((steps, state + 16, wide // 2), BF16),
            pltpu.VMEM((steps, state + 16, wide // 2), BF16),
            pltpu.VMEM((state, wide // 2), BF16),
            pltpu.VMEM((state, wide // 2), BF16),
            pltpu.VMEM((state, wide), BF16),
            pltpu.VMEM((tok, LANES), F32),
            pltpu.VMEM((tok, wide), BF16),
            pltpu.VMEM((tok, wide), BF16),
            pltpu.VMEM((tok, wide), F32),
            pltpu.VMEM((tok, state), BF16),
            pltpu.VMEM((tok, tok), F32),
            pltpu.VMEM((tok, wide), F32),
            pltpu.VMEM((tok, wide), BF16),
            pltpu.VMEM((4, 8, own), F32),
            pltpu.VMEM((4, 8, own), F32),
            pltpu.VMEM((2, own, model), BF16),
            pltpu.VMEM((2, own, model), BF16),
            pltpu.VMEM((own, model), BF16),
            pltpu.VMEM((own, model), BF16),
            pltpu.SemaphoreType.DMA((3, n)),
            pltpu.SemaphoreType.DMA((3, n)),
            pltpu.SemaphoreType.DMA((steps + 3,)),
            pltpu.SemaphoreType.DMA((steps + 3,)),
            pltpu.SemaphoreType.DMA((6,)),
            pltpu.SemaphoreType.DMA((6,)),
        ],
        compiler_params=pltpu.CompilerParams(
            collective_id=0, has_side_effects=True, vmem_limit_bytes=61 * 1024 * 1024
        ),
        name="layer",
    )(
        row_target.reshape(1, tok),
        doc_lengths,
        skip_gain,
        features_in,
        gate_in,
        b_input,
        c_input,
        log_decay.T,
        norm_gain,
        out_weight,
    )


def solution(mesh):
    in_specs = (
        P("seq", "head"),
        P("seq", "head"),
        P("seq", None),
        P("seq", None),
        P("seq", "head"),
        P("seq"),
        P(),
        P("head"),
        P("head"),
        P("head", None),
    )
    out_specs = P(("seq", "head"), None)
    return jax.shard_map(body, mesh=mesh, in_specs=in_specs, out_specs=out_specs, check_vma=False)
```

```python
import functools

import jax
import jax.numpy as jnp
from jax import lax
from jax.experimental import pallas as pl
from jax.experimental.pallas import tpu as pltpu
from jax.sharding import PartitionSpec as P

ATTENTION_LANES = 48
HEAD_DIM = 64
NORM_EPS = 1e-05
LANES = 128
F32 = jnp.float32
BF16 = jnp.bfloat16
MESH = pl.DeviceIdType.MESH


def iota(shape, axis):
    return lax.broadcasted_iota(jnp.int32, shape, axis)


def dot(a, b):
    return jnp.dot(a, b, preferred_element_type=F32)


def dot_nt(a, b):
    return lax.dot_general(a, b, (((1,), (1,)), ((), ())), preferred_element_type=F32)


def layer_kernel(
    n,
    gaps,
    heads,
    docs,
    target_ref,
    doc_ref,
    skip_ref,
    x_hbm,
    z_hbm,
    b_hbm,
    c_hbm,
    small_ref,
    gain_ref,
    w_hbm,
    out_ref,
    x_ref,
    z_ref,
    b_ref,
    c_ref,
    w_ref,
    small_f,
    load_sem,
    send_bc,
    recv_bc,
    bc_out_sem,
    bc_in_sem,
    share_sem,
    send_aux,
    send_x,
    send_z,
    recv_aux,
    recv_x,
    recv_z,
    pair_send,
    pair_recv,
    state_send,
    state_recv,
    last_send,
    last_recv,
    entry_ref,
    opening_ref,
    xs_ref,
    xw_ref,
    zs_ref,
    cs_ref,
    gm_ref,
    mixed_ref,
    gs_ref,
    sq_ref,
    sq_recv,
    a_send,
    a_recv,
    y_send,
    y_recv,
    out_sem,
    in_sem,
    state_out_sem,
    state_in_sem,
    head_out_sem,
    head_in_sem,
):
    tok, wide = x_ref.shape
    cap = tok // n
    state = b_ref.shape[1]
    pairs = wide // LANES
    half = tok // 2
    own = tok // 4
    me = lax.axis_index("seq")
    hd = lax.axis_index("head")
    core, side = hd % 2, hd // 2
    core_peer = side * 2 + (1 - core)
    side_peer = (1 - side) * 2 + core

    column = me % 2
    pair_peer = me + 1 - 2 * column
    loads = [
        pltpu.make_async_copy(src, dst, load_sem.at[i])
        for i, (src, dst) in enumerate(
            (
                (b_hbm, b_ref),
                (c_hbm, c_ref),
                (x_hbm, x_ref),
                (z_hbm, z_ref),
                (w_hbm, w_ref),
            )
        )
    ]
    for load in loads:
        load.start()

    barrier = pltpu.get_barrier_semaphore()

    def greet(k, carry):
        pl.semaphore_signal(
            barrier, inc=1, device_id={"seq": (me + k) % n}, device_id_type=MESH
        )
        return carry

    lax.fori_loop(1, n, greet, 0)
    for k in range(1, 4):
        pl.semaphore_signal(
            barrier, inc=1, device_id={"head": (hd + k) % 4}, device_id_type=MESH
        )

    target = target_ref[...]
    owner = target // tok
    place = target - owner * tok
    far = (owner - me + n) % n
    groups = max(n, 16)
    hits = (iota((groups, tok), 0) == far).astype(F32)
    before = (iota((tok, tok), 0) < iota((tok, tok), 1)).astype(F32).astype(BF16)
    rank = jnp.sum(dot(hits.astype(BF16), before) * hits, axis=0, keepdims=True)
    slot = far * cap + rank.astype(jnp.int32)
    perm = (iota((tok, tok), 0) == slot).astype(F32).astype(BF16)
    high = place // 16
    small_f[...] = jnp.zeros_like(small_f)
    small_f[0:heads] = small_ref[...].astype(F32)
    small_f[heads : heads + 1] = high.astype(F32)
    small_f[heads + 1 : heads + 2] = (place - high * 16).astype(F32)
    small_t = small_f[...].astype(BF16)

    def copy_of(which, send, recv, k):
        return pltpu.make_async_remote_copy(
            src_ref=send.at[k],
            dst_ref=recv.at[k],
            send_sem=out_sem.at[which, k],
            recv_sem=in_sem.at[which, k],
            device_id={"seq": (me + k) % n},
            device_id_type=MESH,
        )

    def start_all(which, send, recv, first, last):
        def go(k, carry):
            copy_of(which, send, recv, k).start()
            return carry

        lax.fori_loop(first, last, go, 0)

    def wait_in(which, send, recv):
        def go(k, carry):
            copy_of(which, send, recv, k).wait_recv()
            return carry

        lax.fori_loop(1, n, go, 0)

    def wait_out(which, send, recv):
        def go(k, carry):
            copy_of(which, send, recv, k).wait_send()
            return carry

        lax.fori_loop(1, n, go, 0)

    def by_slot(values):
        return values.reshape(values.shape[0] // cap, cap, values.shape[1]).astype(BF16)

    def packed_rows(ref):
        if cap % 16 == 0:
            return ref[...].reshape(tok, ref.shape[2])
        return ref[...].astype(F32).reshape(tok, ref.shape[2]).astype(BF16)

    def bc_copy(k):
        return pltpu.make_async_remote_copy(
            src_ref=send_bc.at[k],
            dst_ref=recv_bc.at[k],
            send_sem=bc_out_sem.at[k],
            recv_sem=bc_in_sem.at[k],
            device_id={"seq": (me + k) % n},
            device_id_type=MESH,
        )

    def bc_share(i, p):
        k = hd + 4 * i
        return pltpu.make_async_remote_copy(
            src_ref=recv_bc.at[k],
            dst_ref=recv_bc.at[k],
            send_sem=share_sem.at[i, p],
            recv_sem=bc_in_sem.at[k],
            device_id={"head": (hd + p) % 4},
            device_id_type=MESH,
        )

    def mine(act):
        def go(i, carry):
            @pl.when(hd + 4 * i >= 1)
            def _():
                act(i, hd + 4 * i)

            return carry

        lax.fori_loop(0, n // 4, go, 0)

    loads[0].wait()
    loads[1].wait()
    send_bc[:, :, 0:state] = by_slot(dot(perm, b_ref[...]))
    send_bc[:, :, state:] = by_slot(dot(perm, c_ref[...]))
    send_aux[...] = by_slot(dot_nt(perm, small_t))
    pl.semaphore_wait(barrier, n - 1 + 3)
    mine(lambda i, k: bc_copy(k).start())
    start_all(0, send_aux, recv_aux, 1, n)
    recv_aux[0] = send_aux[0]
    recv_bc[0] = send_bc[0]
    loads[2].wait()
    for part in range(2):
        lo, hi = part * n // 2, (part + 1) * n // 2
        send_x[lo:hi] = by_slot(dot(perm[lo * cap : hi * cap], x_ref[...]))
        start_all(1, send_x, recv_x, max(lo, 1), hi)
    recv_x[0] = send_x[0]
    loads[3].wait()
    send_z[...] = by_slot(dot(perm, z_ref[...]))
    start_all(2, send_z, recv_z, 1, n // 2)
    recv_z[0] = send_z[0]

    first_place = me * tok
    col = iota((tok, 1), 0)
    line = iota((1, tok), 1)
    doc_col = jnp.zeros((tok, 1), jnp.int32)
    doc_line = jnp.zeros((1, tok), jnp.int32)
    doc_last = jnp.int32(0)
    doc_before = jnp.int32(0)
    start = jnp.int32(0)
    for k in range(docs):
        doc_col += jnp.where(col + first_place >= start, 1, 0)
        doc_line += jnp.where(line + first_place >= start, 1, 0)
        doc_last += jnp.where(first_place + tok - 1 >= start, 1, 0)
        doc_before += jnp.where(first_place - 1 >= start, 1, 0)
        start = start + doc_ref[k]
    low = iota((tok, tok), 0) >= iota((tok, tok), 1)
    lane = iota((1, LANES), 1)
    left = lane < HEAD_DIM

    def share(i, k):
        bc_copy(k).wait_recv()
        for p in range(1, 4):
            bc_share(i, p).start()

    mine(share)
    wait_in(0, send_aux, recv_aux)
    aux = packed_rows(recv_aux)
    small_back = aux.astype(F32).T
    places = small_back[heads : heads + 1] * 16.0 + small_back[heads + 1 : heads + 2]
    unperm = (iota((tok, tok), 0) == places.astype(jnp.int32)).astype(F32).astype(BF16)
    aux = dot(unperm, aux)

    def shared(k, carry):
        @pl.when(k % 4 != hd)
        def _():
            bc_copy(k).wait_recv()

        return carry

    lax.fori_loop(1, n, shared, 0)
    both = dot(unperm, packed_rows(recv_bc))
    b_t = both[:, 0:state].T.astype(BF16)
    cs_ref[...] = both[:, state:].astype(BF16)
    decays = jnp.where(lane < heads, aux, 0.0).astype(BF16)
    running = dot(low.astype(F32).astype(BF16), decays)
    running_t = running.T
    closing = running[tok - 1 : tok]
    weight = jnp.exp(closing - running) * jnp.where(doc_col == doc_last, 1.0, 0.0)
    opening_ref[...] = jnp.exp(running) * jnp.where(doc_col == doc_before, 1.0, 0.0)
    through = jnp.exp(closing) * jnp.where(doc_last == doc_before, 1.0, 0.0)
    allowed = low & (doc_col == doc_line)
    gm_ref[...] = jnp.where(allowed, dot(cs_ref[...], b_t), 0.0)

    def spread(values, j):
        return jnp.where(left, values[:, 2 * j : 2 * j + 1], values[:, 2 * j + 1 : 2 * j + 2])

    wait_in(1, send_x, recv_x)
    xs_ref[...] = dot(unperm, packed_rows(recv_x)).astype(BF16)
    for j in range(pairs):
        cols = slice(j * LANES, (j + 1) * LANES)
        xw_ref[:, cols] = (xs_ref[:, cols].astype(F32) * spread(weight, j)).astype(BF16)
    held = dot(b_t, xw_ref[...])
    kept = jnp.concatenate([spread(through, j) for j in range(pairs)], axis=1)

    def fill(ref, held, kept):
        ref[0:state] = held.astype(BF16)
        upper = kept.astype(BF16).astype(F32)
        rows = iota((16, kept.shape[1]), 0)
        ref[state:] = jnp.where(
            rows == 0, upper, jnp.where(rows == 1, kept - upper, 0.0)
        ).astype(BF16)

    def read(ref):
        tail = ref[state:].astype(F32)
        return ref[0:state].astype(F32), tail[0:1] + tail[1:2]

    def pair_copy(which, src, dst, sem):
        return pltpu.make_async_remote_copy(
            src_ref=src,
            dst_ref=dst,
            send_sem=state_out_sem.at[sem],
            recv_sem=state_in_sem.at[which],
            device_id={"seq": pair_peer},
            device_id_type=MESH,
        )

    def state_copy(step):
        return pltpu.make_async_remote_copy(
            src_ref=state_send.at[step],
            dst_ref=state_recv.at[step],
            send_sem=state_out_sem.at[3 + step],
            recv_sem=state_in_sem.at[3 + step],
            device_id={"seq": (me + 2 * gaps[step]) % n},
            device_id_type=MESH,
        )

    def state_start(step, held, kept):
        fill(state_send.at[step], held, kept)

        @pl.when(me + 2 * gaps[step] < n)
        def _():
            state_copy(step).start()

    def state_finish(step):
        @pl.when(me >= 2 * gaps[step])
        def _():
            state_copy(step).wait_recv()

        @pl.when(me < 2 * gaps[step])
        def _():
            state_recv[step] = jnp.zeros(state_recv.shape[1:], BF16)

        return read(state_recv.at[step])

    def inner(j):
        cols = slice(j * LANES, (j + 1) * LANES)
        skip = jnp.where(left, skip_ref[2 * j], skip_ref[2 * j + 1])
        for t0 in range(0, tok, half):
            rows = slice(t0, t0 + half)
            upto = t0 + half
            keys = xs_ref[0:upto, cols]
            sums = []
            for h in (2 * j, 2 * j + 1):
                gaps = jnp.minimum(
                    running[rows, h : h + 1] - running_t[h : h + 1, 0:upto], 0.0
                )
                scores = (gm_ref[rows, 0:upto] * jnp.exp(gaps)).astype(BF16)
                sums.append(dot(scores, keys))
            mixed_ref[rows, cols] = (
                jnp.where(left, sums[0], sums[1]) + skip * xs_ref[rows, cols].astype(F32)
            )

    stages = len(gaps) + 2

    def inner_of(stage):
        for j in range(pairs * stage // stages, pairs * (stage + 1) // stages):
            inner(j)

    part = wide // 2

    def half_copy(which):
        return pair_copy(which, pair_send.at[which], pair_recv.at[which], which)

    last_copy = pair_copy(2, last_send, last_recv, 2)
    for i in range(2):
        fill(pair_send.at[i], held[:, i * part : (i + 1) * part], kept[:, i * part : (i + 1) * part])
    half_copy(1 - column).start()
    half_copy(column).start()
    inner_of(0)
    half_copy(column).wait_recv()
    other, other_kept = read(pair_recv.at[column])

    def ordered(own_one, other_one):
        early = jnp.where(column == 0, own_one, other_one)
        late = jnp.where(column == 0, other_one, own_one)
        return early, late

    def my_half(values):
        return jnp.where(column == 0, values[:, 0:part], values[:, part:])

    early, late = ordered(my_half(held), other)
    early_kept, late_kept = ordered(my_half(kept), other_kept)
    sent, sent_kept = late + late_kept * early, late_kept * early_kept
    for step in range(len(gaps)):
        state_start(step, sent, sent_kept)
        if step == 0:
            start_all(2, send_z, recv_z, n // 2, n)
        inner_of(1 + step)
        came, came_kept = state_finish(step)
        if step > 0:
            came, came_kept = sent + sent_kept * came, sent_kept * came_kept
        sent, sent_kept = came, came_kept
    last_send[...] = sent.astype(BF16)
    last_copy.start()
    inner_of(stages - 1)
    wait_in(2, send_z, recv_z)
    gate = dot(unperm, packed_rows(recv_z))
    zs_ref[...] = gate / (1.0 + jnp.exp(-gate))
    last_copy.wait_recv()
    early, late = ordered(last_send[...].astype(F32), last_recv[...].astype(F32))
    half_copy(1 - column).wait_recv()
    for i, came in enumerate((early, late)):
        other, other_kept = read(pair_recv.at[i])
        came = jnp.where(column == 0, came, other + other_kept * came)
        entry_ref[:, i * part : (i + 1) * part] = came.astype(BF16)

    def gate_rows(where_side, where_core):
        at = where_side * 2 + where_core
        rows = pl.ds(pl.multiple_of(at * own, own), own)
        share = opening_ref[rows, :]
        share = jnp.concatenate([spread(share, j) for j in range(pairs)], axis=1)
        gated = mixed_ref[rows, :] + dot(cs_ref[rows, :], entry_ref[...]) * share
        gated = gated * zs_ref[rows, :]
        gs_ref[rows, :] = (gated * gain_ref[...].reshape(1, wide)).astype(BF16)
        squares = jnp.sum(gated * gated, axis=1, keepdims=True)
        squares = jnp.broadcast_to(squares, (own, LANES)).T[0:8]
        sq_ref[pl.ds(at, 1)] = squares[None]

    def partial(where_side, where_core):
        at = (where_side * 2 + where_core) * own
        return dot(gs_ref[pl.ds(pl.multiple_of(at, own), own), :], w_ref[...])

    def head_copy(which, src, dst, peer):
        return pltpu.make_async_remote_copy(
            src_ref=src,
            dst_ref=dst,
            send_sem=head_out_sem.at[which],
            recv_sem=head_in_sem.at[which],
            device_id={"head": peer},
            device_id_type=MESH,
        )

    loads[4].wait()
    copies = [head_copy(i, a_send.at[i], a_recv.at[i], core_peer) for i in range(2)]
    across = head_copy(2, y_send, y_recv, side_peer)
    gate_rows(1 - side, 1 - core)
    a_send[0] = partial(1 - side, 1 - core).astype(BF16)
    copies[0].start()
    gate_rows(1 - side, core)
    passing = partial(1 - side, core)
    copies[0].wait_recv()
    y_send[...] = (passing + a_recv[0].astype(F32)).astype(BF16)
    across.start()
    gate_rows(side, 1 - core)
    a_send[1] = partial(side, 1 - core).astype(BF16)
    copies[1].start()
    gate_rows(side, core)
    sq_copies = [
        head_copy(2 + k, sq_ref.at[(hd + k) % 4], sq_recv.at[k], (hd + k) % 4) for k in range(1, 4)
    ]
    for copy in sq_copies:
        copy.start()
    total = partial(side, core)
    for copy in sq_copies:
        copy.wait_recv()
    squares = sq_ref[pl.ds(hd, 1)][0] + sq_recv[1] + sq_recv[2] + sq_recv[3]
    scale = lax.rsqrt(squares / (ATTENTION_LANES * HEAD_DIM) + NORM_EPS)
    scale = jnp.broadcast_to(scale[0:1], (LANES, own)).T[:, 0:1]
    copies[1].wait_recv()
    total = total + a_recv[1].astype(F32)
    across.wait_recv()
    out_ref[...] = ((total + y_recv[...].astype(F32)) * scale).astype(BF16)

    wait_out(0, send_aux, recv_aux)
    wait_out(1, send_x, recv_x)
    wait_out(2, send_z, recv_z)
    mine(lambda i, k: bc_copy(k).wait_send())

    def shared_out(i, k):
        for p in range(1, 4):
            bc_share(i, p).wait_send()

    mine(shared_out)
    for i in range(2):
        half_copy(i).wait_send()
    last_copy.wait_send()
    for step in range(len(gaps)):

        @pl.when(me + 2 * gaps[step] < n)
        def _():
            state_copy(step).wait_send()

    for copy in copies + [across] + sq_copies:
        copy.wait_send()


def body(
    features_in,
    gate_in,
    b_input,
    c_input,
    log_decay,
    row_target,
    doc_lengths,
    skip_gain,
    norm_gain,
    out_weight,
):
    tok, wide = features_in.shape
    heads = log_decay.shape[1]
    state = b_input.shape[1]
    model = out_weight.shape[1]
    n = lax.axis_size("seq")
    cap = tok // n
    aux = LANES
    gaps, reach = [1], 1
    while reach < n // 4:
        gaps, reach = gaps + [reach], reach * 2
    steps = len(gaps)
    vmem = pl.BlockSpec(memory_space=pltpu.VMEM)
    smem = pl.BlockSpec(memory_space=pltpu.SMEM)
    hbm = pl.BlockSpec(memory_space=pltpu.HBM)
    own = tok // 4
    kernel = functools.partial(layer_kernel, n, gaps, heads, doc_lengths.shape[0])
    return pl.pallas_call(
        kernel,
        out_shape=jax.ShapeDtypeStruct((own, model), BF16),
        in_specs=[vmem, smem, smem] + [hbm] * 4 + [vmem] * 2 + [hbm],
        out_specs=vmem,
        scratch_shapes=[
            pltpu.VMEM((tok, wide), BF16),
            pltpu.VMEM((tok, wide), BF16),
            pltpu.VMEM((tok, state), BF16),
            pltpu.VMEM((tok, state), BF16),
            pltpu.VMEM((wide, model), BF16),
            pltpu.VMEM((LANES, tok), F32),
            pltpu.SemaphoreType.DMA((5,)),
            pltpu.VMEM((n, cap, 2 * state), BF16),
            pltpu.VMEM((n, cap, 2 * state), BF16),
            pltpu.SemaphoreType.DMA((n,)),
            pltpu.SemaphoreType.DMA((n,)),
            pltpu.SemaphoreType.DMA((n // 4, 4)),
            pltpu.VMEM((n, cap, aux), BF16),
            pltpu.VMEM((n, cap, wide), BF16),
            pltpu.VMEM((n, cap, wide), BF16),
            pltpu.VMEM((n, cap, aux), BF16),
            pltpu.VMEM((n, cap, wide), BF16),
            pltpu.VMEM((n, cap, wide), BF16),
            pltpu.VMEM((2, state + 16, wide // 2), BF16),
            pltpu.VMEM((2, state + 16, wide // 2), BF16),
            pltpu.VMEM((steps, state + 16, wide // 2), BF16),
            pltpu.VMEM((steps, state + 16, wide // 2), BF16),
            pltpu.VMEM((state, wide // 2), BF16),
            pltpu.VMEM((state, wide // 2), BF16),
            pltpu.VMEM((state, wide), BF16),
            pltpu.VMEM((tok, LANES), F32),
            pltpu.VMEM((tok, wide), BF16),
            pltpu.VMEM((tok, wide), BF16),
            pltpu.VMEM((tok, wide), F32),
            pltpu.VMEM((tok, state), BF16),
            pltpu.VMEM((tok, tok), F32),
            pltpu.VMEM((tok, wide), F32),
            pltpu.VMEM((tok, wide), BF16),
            pltpu.VMEM((4, 8, own), F32),
            pltpu.VMEM((4, 8, own), F32),
            pltpu.VMEM((2, own, model), BF16),
            pltpu.VMEM((2, own, model), BF16),
            pltpu.VMEM((own, model), BF16),
            pltpu.VMEM((own, model), BF16),
            pltpu.SemaphoreType.DMA((3, n)),
            pltpu.SemaphoreType.DMA((3, n)),
            pltpu.SemaphoreType.DMA((steps + 3,)),
            pltpu.SemaphoreType.DMA((steps + 3,)),
            pltpu.SemaphoreType.DMA((6,)),
            pltpu.SemaphoreType.DMA((6,)),
        ],
        compiler_params=pltpu.CompilerParams(
            collective_id=0, has_side_effects=True, vmem_limit_bytes=61 * 1024 * 1024
        ),
        name="layer",
    )(
        row_target.reshape(1, tok),
        doc_lengths,
        skip_gain,
        features_in,
        gate_in,
        b_input,
        c_input,
        log_decay.T,
        norm_gain,
        out_weight,
    )


def solution(mesh):
    in_specs = (
        P("seq", "head"),
        P("seq", "head"),
        P("seq", None),
        P("seq", None),
        P("seq", "head"),
        P("seq"),
        P(),
        P("head"),
        P("head"),
        P("head", None),
    )
    out_specs = P(("seq", "head"), None)
    return jax.shard_map(body, mesh=mesh, in_specs=in_specs, out_specs=out_specs, check_vma=False)
```

```python
import functools

import jax
import jax.numpy as jnp
from jax import lax
from jax.experimental import pallas as pl
from jax.experimental.pallas import tpu as pltpu
from jax.sharding import PartitionSpec as P

ATTENTION_LANES = 48
HEAD_DIM = 64
NORM_EPS = 1e-05
LANES = 128
F32 = jnp.float32
BF16 = jnp.bfloat16
MESH = pl.DeviceIdType.MESH


def iota(shape, axis):
    return lax.broadcasted_iota(jnp.int32, shape, axis)


def dot(a, b):
    return jnp.dot(a, b, preferred_element_type=F32)


def dot_nt(a, b):
    return lax.dot_general(a, b, (((1,), (1,)), ((), ())), preferred_element_type=F32)


def layer_kernel(
    n,
    gaps,
    heads,
    docs,
    target_ref,
    doc_ref,
    skip_ref,
    x_hbm,
    z_hbm,
    b_hbm,
    c_hbm,
    small_ref,
    gain_ref,
    w_hbm,
    out_ref,
    x_ref,
    z_ref,
    b_ref,
    c_ref,
    w_ref,
    small_f,
    load_sem,
    send_bc,
    recv_bc,
    bc_out_sem,
    bc_in_sem,
    share_sem,
    send_aux,
    send_x,
    send_z,
    recv_aux,
    recv_x,
    recv_z,
    pair_send,
    pair_recv,
    state_send,
    state_recv,
    last_send,
    last_recv,
    entry_ref,
    opening_ref,
    xs_ref,
    xw_ref,
    zs_ref,
    cs_ref,
    gm_ref,
    mixed_ref,
    gs_ref,
    sq_ref,
    sq_recv,
    a_send,
    a_recv,
    y_send,
    y_recv,
    out_sem,
    in_sem,
    state_out_sem,
    state_in_sem,
    head_out_sem,
    head_in_sem,
):
    tok, wide = x_ref.shape
    cap = tok // n
    state = b_ref.shape[1]
    pairs = wide // LANES
    half = tok // 2
    own = tok // 4
    me = lax.axis_index("seq")
    hd = lax.axis_index("head")
    core, side = hd % 2, hd // 2
    core_peer = side * 2 + (1 - core)
    side_peer = (1 - side) * 2 + core

    column = me % 2
    pair_peer = me + 1 - 2 * column
    loads = [
        pltpu.make_async_copy(src, dst, load_sem.at[i])
        for i, (src, dst) in enumerate(
            (
                (b_hbm, b_ref),
                (c_hbm, c_ref),
                (x_hbm, x_ref),
                (z_hbm, z_ref),
                (w_hbm, w_ref),
            )
        )
    ]
    for load in loads:
        load.start()

    barrier = pltpu.get_barrier_semaphore()

    def greet(k, carry):
        pl.semaphore_signal(
            barrier, inc=1, device_id={"seq": (me + k) % n}, device_id_type=MESH
        )
        return carry

    lax.fori_loop(1, n, greet, 0)
    for k in range(1, 4):
        pl.semaphore_signal(
            barrier, inc=1, device_id={"head": (hd + k) % 4}, device_id_type=MESH
        )

    target = target_ref[...]
    owner = target // tok
    place = target - owner * tok
    far = (owner - me + n) % n
    groups = max(n, 16)
    hits = (iota((groups, tok), 0) == far).astype(F32)
    before = (iota((tok, tok), 0) < iota((tok, tok), 1)).astype(F32).astype(BF16)
    rank = jnp.sum(dot(hits.astype(BF16), before) * hits, axis=0, keepdims=True)
    slot = far * cap + rank.astype(jnp.int32)
    perm = (iota((tok, tok), 0) == slot).astype(F32).astype(BF16)
    high = place // 16
    small_f[...] = jnp.zeros_like(small_f)
    small_f[0:heads] = small_ref[...].astype(F32)
    small_f[heads : heads + 1] = high.astype(F32)
    small_f[heads + 1 : heads + 2] = (place - high * 16).astype(F32)
    small_t = small_f[...].astype(BF16)

    def copy_of(which, send, recv, k):
        return pltpu.make_async_remote_copy(
            src_ref=send.at[k],
            dst_ref=recv.at[k],
            send_sem=out_sem.at[which, k],
            recv_sem=in_sem.at[which, k],
            device_id={"seq": (me + k) % n},
            device_id_type=MESH,
        )

    def start_all(which, send, recv, first, last):
        def go(k, carry):
            copy_of(which, send, recv, k).start()
            return carry

        lax.fori_loop(first, last, go, 0)

    def wait_in(which, send, recv):
        def go(k, carry):
            copy_of(which, send, recv, k).wait_recv()
            return carry

        lax.fori_loop(1, n, go, 0)

    def wait_out(which, send, recv):
        def go(k, carry):
            copy_of(which, send, recv, k).wait_send()
            return carry

        lax.fori_loop(1, n, go, 0)

    def by_slot(values):
        return values.reshape(values.shape[0] // cap, cap, values.shape[1]).astype(BF16)

    def packed_rows(ref):
        if cap % 16 == 0:
            return ref[...].reshape(tok, ref.shape[2])
        return ref[...].astype(F32).reshape(tok, ref.shape[2]).astype(BF16)

    def bc_copy(k):
        return pltpu.make_async_remote_copy(
            src_ref=send_bc.at[k],
            dst_ref=recv_bc.at[k],
            send_sem=bc_out_sem.at[k],
            recv_sem=bc_in_sem.at[k],
            device_id={"seq": (me + k) % n},
            device_id_type=MESH,
        )

    def bc_share(i, p):
        k = hd + 4 * i
        return pltpu.make_async_remote_copy(
            src_ref=recv_bc.at[k],
            dst_ref=recv_bc.at[k],
            send_sem=share_sem.at[i, p],
            recv_sem=bc_in_sem.at[k],
            device_id={"head": (hd + p) % 4},
            device_id_type=MESH,
        )

    def mine(act):
        def go(i, carry):
            @pl.when(hd + 4 * i >= 1)
            def _():
                act(i, hd + 4 * i)

            return carry

        lax.fori_loop(0, n // 4, go, 0)

    loads[0].wait()
    loads[1].wait()
    send_bc[:, :, 0:state] = by_slot(dot(perm, b_ref[...]))
    send_bc[:, :, state:] = by_slot(dot(perm, c_ref[...]))
    send_aux[...] = by_slot(dot_nt(perm, small_t))
    pl.semaphore_wait(barrier, n - 1 + 3)
    mine(lambda i, k: bc_copy(k).start())
    start_all(0, send_aux, recv_aux, 1, n)
    recv_aux[0] = send_aux[0]
    recv_bc[0] = send_bc[0]
    loads[2].wait()
    for part in range(2):
        lo, hi = part * n // 2, (part + 1) * n // 2
        send_x[lo:hi] = by_slot(dot(perm[lo * cap : hi * cap], x_ref[...]))
        start_all(1, send_x, recv_x, max(lo, 1), hi)
    recv_x[0] = send_x[0]
    loads[3].wait()
    send_z[...] = by_slot(dot(perm, z_ref[...]))
    start_all(2, send_z, recv_z, 1, n)
    recv_z[0] = send_z[0]

    first_place = me * tok
    col = iota((tok, 1), 0)
    line = iota((1, tok), 1)
    doc_col = jnp.zeros((tok, 1), jnp.int32)
    doc_line = jnp.zeros((1, tok), jnp.int32)
    doc_last = jnp.int32(0)
    doc_before = jnp.int32(0)
    start = jnp.int32(0)
    for k in range(docs):
        doc_col += jnp.where(col + first_place >= start, 1, 0)
        doc_line += jnp.where(line + first_place >= start, 1, 0)
        doc_last += jnp.where(first_place + tok - 1 >= start, 1, 0)
        doc_before += jnp.where(first_place - 1 >= start, 1, 0)
        start = start + doc_ref[k]
    low = iota((tok, tok), 0) >= iota((tok, tok), 1)
    lane = iota((1, LANES), 1)
    left = lane < HEAD_DIM

    def share(i, k):
        bc_copy(k).wait_recv()
        for p in range(1, 4):
            bc_share(i, p).start()

    mine(share)
    wait_in(0, send_aux, recv_aux)
    aux = packed_rows(recv_aux)
    small_back = aux.astype(F32).T
    places = small_back[heads : heads + 1] * 16.0 + small_back[heads + 1 : heads + 2]
    unperm = (iota((tok, tok), 0) == places.astype(jnp.int32)).astype(F32).astype(BF16)
    aux = dot(unperm, aux)

    def shared(k, carry):
        @pl.when(k % 4 != hd)
        def _():
            bc_copy(k).wait_recv()

        return carry

    lax.fori_loop(1, n, shared, 0)
    both = dot(unperm, packed_rows(recv_bc))
    b_t = both[:, 0:state].T.astype(BF16)
    cs_ref[...] = both[:, state:].astype(BF16)
    decays = jnp.where(lane < heads, aux, 0.0).astype(BF16)
    running = dot(low.astype(F32).astype(BF16), decays)
    running_t = running.T
    closing = running[tok - 1 : tok]
    weight = jnp.exp(closing - running) * jnp.where(doc_col == doc_last, 1.0, 0.0)
    opening_ref[...] = jnp.exp(running) * jnp.where(doc_col == doc_before, 1.0, 0.0)
    through = jnp.exp(closing) * jnp.where(doc_last == doc_before, 1.0, 0.0)
    allowed = low & (doc_col == doc_line)
    gm_ref[...] = jnp.where(allowed, dot(cs_ref[...], b_t), 0.0)

    def spread(values, j):
        return jnp.where(left, values[:, 2 * j : 2 * j + 1], values[:, 2 * j + 1 : 2 * j + 2])

    wait_in(1, send_x, recv_x)
    xs_ref[...] = dot(unperm, packed_rows(recv_x)).astype(BF16)
    for j in range(pairs):
        cols = slice(j * LANES, (j + 1) * LANES)
        xw_ref[:, cols] = (xs_ref[:, cols].astype(F32) * spread(weight, j)).astype(BF16)
    held = dot(b_t, xw_ref[...])
    kept = jnp.concatenate([spread(through, j) for j in range(pairs)], axis=1)

    def fill(ref, held, kept):
        ref[0:state] = held.astype(BF16)
        upper = kept.astype(BF16).astype(F32)
        rows = iota((16, kept.shape[1]), 0)
        ref[state:] = jnp.where(
            rows == 0, upper, jnp.where(rows == 1, kept - upper, 0.0)
        ).astype(BF16)

    def read(ref):
        tail = ref[state:].astype(F32)
        return ref[0:state].astype(F32), tail[0:1] + tail[1:2]

    def pair_copy(which, src, dst, sem):
        return pltpu.make_async_remote_copy(
            src_ref=src,
            dst_ref=dst,
            send_sem=state_out_sem.at[sem],
            recv_sem=state_in_sem.at[which],
            device_id={"seq": pair_peer},
            device_id_type=MESH,
        )

    def state_copy(step):
        return pltpu.make_async_remote_copy(
            src_ref=state_send.at[step],
            dst_ref=state_recv.at[step],
            send_sem=state_out_sem.at[3 + step],
            recv_sem=state_in_sem.at[3 + step],
            device_id={"seq": (me + 2 * gaps[step]) % n},
            device_id_type=MESH,
        )

    def state_start(step, held, kept):
        fill(state_send.at[step], held, kept)

        @pl.when(me + 2 * gaps[step] < n)
        def _():
            state_copy(step).start()

    def state_finish(step):
        @pl.when(me >= 2 * gaps[step])
        def _():
            state_copy(step).wait_recv()

        @pl.when(me < 2 * gaps[step])
        def _():
            state_recv[step] = jnp.zeros(state_recv.shape[1:], BF16)

        return read(state_recv.at[step])

    def inner(j):
        cols = slice(j * LANES, (j + 1) * LANES)
        skip = jnp.where(left, skip_ref[2 * j], skip_ref[2 * j + 1])
        for t0 in range(0, tok, own):
            rows = slice(t0, t0 + own)
            upto = t0 + own
            keys = xs_ref[0:upto, cols]
            sums = []
            for h in (2 * j, 2 * j + 1):
                gaps = jnp.minimum(
                    running[rows, h : h + 1] - running_t[h : h + 1, 0:upto], 0.0
                )
                scores = (gm_ref[rows, 0:upto] * jnp.exp(gaps)).astype(BF16)
                sums.append(dot(scores, keys))
            mixed_ref[rows, cols] = (
                jnp.where(left, sums[0], sums[1]) + skip * xs_ref[rows, cols].astype(F32)
            )

    stages = len(gaps) + 2

    def inner_of(stage):
        for j in range(pairs * stage // stages, pairs * (stage + 1) // stages):
            inner(j)

    part = wide // 2

    def half_copy(which):
        return pair_copy(which, pair_send.at[which], pair_recv.at[which], which)

    last_copy = pair_copy(2, last_send, last_recv, 2)
    for i in range(2):
        fill(pair_send.at[i], held[:, i * part : (i + 1) * part], kept[:, i * part : (i + 1) * part])
    half_copy(1 - column).start()
    half_copy(column).start()
    inner_of(0)
    half_copy(column).wait_recv()
    other, other_kept = read(pair_recv.at[column])

    def ordered(own_one, other_one):
        early = jnp.where(column == 0, own_one, other_one)
        late = jnp.where(column == 0, other_one, own_one)
        return early, late

    def my_half(values):
        return jnp.where(column == 0, values[:, 0:part], values[:, part:])

    early, late = ordered(my_half(held), other)
    early_kept, late_kept = ordered(my_half(kept), other_kept)
    sent, sent_kept = late + late_kept * early, late_kept * early_kept
    for step in range(len(gaps)):
        state_start(step, sent, sent_kept)
        inner_of(1 + step)
        came, came_kept = state_finish(step)
        if step > 0:
            came, came_kept = sent + sent_kept * came, sent_kept * came_kept
        sent, sent_kept = came, came_kept
    last_send[...] = sent.astype(BF16)
    last_copy.start()
    inner_of(stages - 1)
    wait_in(2, send_z, recv_z)
    gate = dot(unperm, packed_rows(recv_z))
    zs_ref[...] = gate / (1.0 + jnp.exp(-gate))
    last_copy.wait_recv()
    early, late = ordered(last_send[...].astype(F32), last_recv[...].astype(F32))
    half_copy(1 - column).wait_recv()
    for i, came in enumerate((early, late)):
        other, other_kept = read(pair_recv.at[i])
        came = jnp.where(column == 0, came, other + other_kept * came)
        entry_ref[:, i * part : (i + 1) * part] = came.astype(BF16)

    def gate_rows(where_side, where_core):
        at = where_side * 2 + where_core
        rows = pl.ds(pl.multiple_of(at * own, own), own)
        share = opening_ref[rows, :]
        share = jnp.concatenate([spread(share, j) for j in range(pairs)], axis=1)
        gated = mixed_ref[rows, :] + dot(cs_ref[rows, :], entry_ref[...]) * share
        gated = gated * zs_ref[rows, :]
        gs_ref[rows, :] = (gated * gain_ref[...].reshape(1, wide)).astype(BF16)
        squares = jnp.sum(gated * gated, axis=1, keepdims=True)
        squares = jnp.broadcast_to(squares, (own, LANES)).T[0:8]
        sq_ref[pl.ds(at, 1)] = squares[None]

    def partial(where_side, where_core):
        at = (where_side * 2 + where_core) * own
        return dot(gs_ref[pl.ds(pl.multiple_of(at, own), own), :], w_ref[...])

    def head_copy(which, src, dst, peer):
        return pltpu.make_async_remote_copy(
            src_ref=src,
            dst_ref=dst,
            send_sem=head_out_sem.at[which],
            recv_sem=head_in_sem.at[which],
            device_id={"head": peer},
            device_id_type=MESH,
        )

    loads[4].wait()
    copies = [head_copy(i, a_send.at[i], a_recv.at[i], core_peer) for i in range(2)]
    across = head_copy(2, y_send, y_recv, side_peer)
    gate_rows(1 - side, 1 - core)
    a_send[0] = partial(1 - side, 1 - core).astype(BF16)
    copies[0].start()
    gate_rows(1 - side, core)
    passing = partial(1 - side, core)
    copies[0].wait_recv()
    y_send[...] = (passing + a_recv[0].astype(F32)).astype(BF16)
    across.start()
    gate_rows(side, 1 - core)
    a_send[1] = partial(side, 1 - core).astype(BF16)
    copies[1].start()
    gate_rows(side, core)
    sq_copies = [
        head_copy(2 + k, sq_ref.at[(hd + k) % 4], sq_recv.at[k], (hd + k) % 4) for k in range(1, 4)
    ]
    for copy in sq_copies:
        copy.start()
    total = partial(side, core)
    for copy in sq_copies:
        copy.wait_recv()
    squares = sq_ref[pl.ds(hd, 1)][0] + sq_recv[1] + sq_recv[2] + sq_recv[3]
    scale = lax.rsqrt(squares / (ATTENTION_LANES * HEAD_DIM) + NORM_EPS)
    scale = jnp.broadcast_to(scale[0:1], (LANES, own)).T[:, 0:1]
    copies[1].wait_recv()
    total = total + a_recv[1].astype(F32)
    across.wait_recv()
    out_ref[...] = ((total + y_recv[...].astype(F32)) * scale).astype(BF16)

    wait_out(0, send_aux, recv_aux)
    wait_out(1, send_x, recv_x)
    wait_out(2, send_z, recv_z)
    mine(lambda i, k: bc_copy(k).wait_send())

    def shared_out(i, k):
        for p in range(1, 4):
            bc_share(i, p).wait_send()

    mine(shared_out)
    for i in range(2):
        half_copy(i).wait_send()
    last_copy.wait_send()
    for step in range(len(gaps)):

        @pl.when(me + 2 * gaps[step] < n)
        def _():
            state_copy(step).wait_send()

    for copy in copies + [across] + sq_copies:
        copy.wait_send()


def body(
    features_in,
    gate_in,
    b_input,
    c_input,
    log_decay,
    row_target,
    doc_lengths,
    skip_gain,
    norm_gain,
    out_weight,
):
    tok, wide = features_in.shape
    heads = log_decay.shape[1]
    state = b_input.shape[1]
    model = out_weight.shape[1]
    n = lax.axis_size("seq")
    cap = tok // n
    aux = LANES
    gaps, reach = [1], 1
    while reach < n // 4:
        gaps, reach = gaps + [reach], reach * 2
    steps = len(gaps)
    vmem = pl.BlockSpec(memory_space=pltpu.VMEM)
    smem = pl.BlockSpec(memory_space=pltpu.SMEM)
    hbm = pl.BlockSpec(memory_space=pltpu.HBM)
    own = tok // 4
    kernel = functools.partial(layer_kernel, n, gaps, heads, doc_lengths.shape[0])
    return pl.pallas_call(
        kernel,
        out_shape=jax.ShapeDtypeStruct((own, model), BF16),
        in_specs=[vmem, smem, smem] + [hbm] * 4 + [vmem] * 2 + [hbm],
        out_specs=vmem,
        scratch_shapes=[
            pltpu.VMEM((tok, wide), BF16),
            pltpu.VMEM((tok, wide), BF16),
            pltpu.VMEM((tok, state), BF16),
            pltpu.VMEM((tok, state), BF16),
            pltpu.VMEM((wide, model), BF16),
            pltpu.VMEM((LANES, tok), F32),
            pltpu.SemaphoreType.DMA((5,)),
            pltpu.VMEM((n, cap, 2 * state), BF16),
            pltpu.VMEM((n, cap, 2 * state), BF16),
            pltpu.SemaphoreType.DMA((n,)),
            pltpu.SemaphoreType.DMA((n,)),
            pltpu.SemaphoreType.DMA((n // 4, 4)),
            pltpu.VMEM((n, cap, aux), BF16),
            pltpu.VMEM((n, cap, wide), BF16),
            pltpu.VMEM((n, cap, wide), BF16),
            pltpu.VMEM((n, cap, aux), BF16),
            pltpu.VMEM((n, cap, wide), BF16),
            pltpu.VMEM((n, cap, wide), BF16),
            pltpu.VMEM((2, state + 16, wide // 2), BF16),
            pltpu.VMEM((2, state + 16, wide // 2), BF16),
            pltpu.VMEM((steps, state + 16, wide // 2), BF16),
            pltpu.VMEM((steps, state + 16, wide // 2), BF16),
            pltpu.VMEM((state, wide // 2), BF16),
            pltpu.VMEM((state, wide // 2), BF16),
            pltpu.VMEM((state, wide), BF16),
            pltpu.VMEM((tok, LANES), F32),
            pltpu.VMEM((tok, wide), BF16),
            pltpu.VMEM((tok, wide), BF16),
            pltpu.VMEM((tok, wide), F32),
            pltpu.VMEM((tok, state), BF16),
            pltpu.VMEM((tok, tok), F32),
            pltpu.VMEM((tok, wide), F32),
            pltpu.VMEM((tok, wide), BF16),
            pltpu.VMEM((4, 8, own), F32),
            pltpu.VMEM((4, 8, own), F32),
            pltpu.VMEM((2, own, model), BF16),
            pltpu.VMEM((2, own, model), BF16),
            pltpu.VMEM((own, model), BF16),
            pltpu.VMEM((own, model), BF16),
            pltpu.SemaphoreType.DMA((3, n)),
            pltpu.SemaphoreType.DMA((3, n)),
            pltpu.SemaphoreType.DMA((steps + 3,)),
            pltpu.SemaphoreType.DMA((steps + 3,)),
            pltpu.SemaphoreType.DMA((6,)),
            pltpu.SemaphoreType.DMA((6,)),
        ],
        compiler_params=pltpu.CompilerParams(
            collective_id=0, has_side_effects=True, vmem_limit_bytes=61 * 1024 * 1024
        ),
        name="layer",
    )(
        row_target.reshape(1, tok),
        doc_lengths,
        skip_gain,
        features_in,
        gate_in,
        b_input,
        c_input,
        log_decay.T,
        norm_gain,
        out_weight,
    )


def solution(mesh):
    in_specs = (
        P("seq", "head"),
        P("seq", "head"),
        P("seq", None),
        P("seq", None),
        P("seq", "head"),
        P("seq"),
        P(),
        P("head"),
        P("head"),
        P("head", None),
    )
    out_specs = P(("seq", "head"), None)
    return jax.shard_map(body, mesh=mesh, in_specs=in_specs, out_specs=out_specs, check_vma=False)
```
